32 devices in a mesh: dp: 8 (over z, x), tensor: 2 (over core), section: 2 (over y).
Axes of the slice: x: 2, y: 2, z: 4, core: 2. Of those that a mesh axis runs over, the one named last changes fastest.
Arguments:
- section_layer_input: bfloat16 [2, 2048, 4096], P('section', ('dp', 'tensor')), may hold values from -6 to 6
- value_projection_weight: bfloat16 [2, 4096, 1024], P('section', 'dp', 'tensor'), may hold values from -0.09375 to 0.09375
- adapter_down_weight: bfloat16 [2, 4096, 16], P('section'), may hold values from -0.09375 to 0.09375
- adapter_up_weight: bfloat16 [2, 16, 1024], P('section', None, 'tensor'), may hold values from -0.75 to 0.75
- output_weight: bfloat16 [2, 4096, 4096], P('section', 'tensor', 'dp'), may hold values from -0.09375 to 0.09375
- rotated_query_cache: bfloat16 [2, 2048, 4096], P('section', 'dp', 'tensor'), may hold values from -500 to 500
- rotated_key_cache: bfloat16 [2, 2048, 1024], P('section', 'dp', 'tensor'), may hold values from -5 to 5
- query_embedding: bfloat16 [8, 4096], P('dp'), may hold values from -6 to 6
- positives: int32 [8], P('dp'), may hold values from 0 to 15, as said below
- hard_negative_passages: int32 [8, 7], P('dp'), may hold values from 0 to 15
- lengths: int32 [16], P('dp'), may hold values from 32 to 128, as said below
Outputs:
- query_loss: float32 [8], P('dp')
- grad_input: bfloat16 [2, 2048, 4096], P('section', ('dp', 'tensor'))
- grad_down: float32 [2, 4096, 16], P('section')
- grad_up: float32 [2, 16, 1024], P('section', None, 'tensor')
The draws below stay inside these ranges and needn't reach their ends.
Inputs may be any that keep to these rules, and one draw needn't show every extreme that they name: `positives`: distinct passage numbers. `lengths`: the first passage uses all 128 tokens.
All inputs are finite; a program needn't handle non-finite values.
Results may differ from the reference program's by a relative error of at most 0.012.
Values may be sent and summed in bfloat16 or wider, within the bound.
A program may use at most 128 MiB of HBM per device.

```python
import math
import jax
import jax.numpy as jnp
from jax import lax

MODEL_WIDTH = 4096
HEAD_SIZE = 128
KEY_VALUE_HEADS = 8
QH = 32
ADAPTER_RANK = 16
LEN = 128
NNEG = 7
TOKENS = 2048
PASSAGES = 16
QUERIES = 8
N_TENSOR = 2


def shared_keys(key):
    base = jax.random.normal(key, (2, PASSAGES, LEN, KEY_VALUE_HEADS, HEAD_SIZE), jnp.float32)
    base = jnp.clip(base, -4.0, 4.0)
    return base.at[:, :, 1].set(base[:, :, 0] * 1.015)


def draw_rotated_key_cache(key, part):
    base = shared_keys(key)
    return base.reshape(2, TOKENS, KEY_VALUE_HEADS * HEAD_SIZE).astype(jnp.bfloat16)


def draw_rotated_query_cache(key, part):
    key = jax.random.fold_in(key, 37)
    noise_key, sharp_key = jax.random.split(key, 2)
    group = QH // KEY_VALUE_HEADS
    head_shape = (2, PASSAGES, 1, KEY_VALUE_HEADS, group, 1)
    noise = jnp.clip(jax.random.normal(noise_key, (2, PASSAGES, LEN, KEY_VALUE_HEADS, group, HEAD_SIZE), jnp.float32), -4.0, 4.0)
    sharpness = jax.random.uniform(sharp_key, head_shape, jnp.float32, 0.5, 2.5)
    queries = noise * sharpness
    return queries.reshape(2, TOKENS, QH * HEAD_SIZE).astype(jnp.bfloat16)


def draw_positives(key, part):
    key = jax.random.fold_in(key, 11)
    order = jax.random.permutation(key, PASSAGES)
    return order[:QUERIES].astype(jnp.int32)


def draw_lengths(key, part):
    key = jax.random.fold_in(key, 23)
    drawn = jax.random.randint(key, (PASSAGES,), LEN // 4, LEN + 1)
    return drawn.at[0].set(LEN).astype(jnp.int32)


def touch_ends(values, rng, smallest, high):
    shape = values.shape
    spot = [jax.random.randint(jax.random.fold_in(rng, axis), (), 0, shape[axis]) for axis in range(len(shape))]
    values = values.at[tuple(spot)].set(smallest)
    longest = shape.index(max(shape))
    spot[longest] = (spot[longest] + 1) % shape[longest]
    return values.at[tuple(spot)].set(high)


def block_levels(rng, shape, shards, low, top_value):
    factor_of, own = 1.0, jax.random.fold_in(rng, 6)
    for dim, parts in shards:
        heights = jnp.exp(jax.random.uniform(jax.random.fold_in(own, dim), (parts,), jnp.float32, low / len(shards), top_value / len(shards)))
        factor_of = factor_of * jnp.repeat(heights, shape[dim] // parts).reshape([-1 if axis == dim else 1 for axis in range(len(shape))])
    return factor_of


def centred(rng, extent, spread, most, shards=(), kind=jnp.bfloat16):
    array = spread * jax.random.normal(rng, extent, jnp.float32)
    if shards:
        array = array * block_levels(rng, extent, shards, -0.22, 0.18)
    return jnp.clip(array, -most, most).astype(kind)


def setup_inputs(seed: int = 0) -> dict:
    keys = jax.random.split(jax.random.key(seed), 12)
    return {
        "section_layer_input": centred(keys[0], (2, TOKENS, MODEL_WIDTH), 1.0, 6.0, ((0, 2), (1, 16))),
        "value_projection_weight": centred(keys[1], (2, MODEL_WIDTH, KEY_VALUE_HEADS * HEAD_SIZE), MODEL_WIDTH ** -0.5, 0.09375, ((0, 2), (1, 8), (2, 2))),
        "adapter_down_weight": centred(keys[2], (2, MODEL_WIDTH, ADAPTER_RANK), MODEL_WIDTH ** -0.5, 0.09375, ((0, 2),)),
        "adapter_up_weight": centred(keys[3], (2, ADAPTER_RANK, KEY_VALUE_HEADS * HEAD_SIZE), (4 * ADAPTER_RANK) ** -0.5, 0.75, ((0, 2), (2, 2))),
        "output_weight": centred(keys[4], (2, QH * HEAD_SIZE, MODEL_WIDTH), (QH * HEAD_SIZE) ** -0.5, 0.09375, ((0, 2), (1, 2), (2, 8))),
        "rotated_query_cache": draw_rotated_query_cache(jax.random.fold_in(keys[11], 71), 0),
        "rotated_key_cache": draw_rotated_key_cache(jax.random.fold_in(keys[11], 71), 0),
        "query_embedding": centred(keys[7], (QUERIES, MODEL_WIDTH), 1.0, 6.0, ((0, 8),)),
        "positives": draw_positives(jax.random.fold_in(keys[11], 71), 0),
        "hard_negative_passages": touch_ends(jax.random.randint(keys[9], (QUERIES, NNEG), 0, PASSAGES), jax.random.fold_in(keys[9], 1), 0, PASSAGES - 1).astype(jnp.int32),
        "lengths": draw_lengths(jax.random.fold_in(keys[11], 71), 0),
    }


tau_value = 0.02
adapter_scale = 2.0
loss_scale = 65536.0
tiny_eps = 1e-06
very_low = -1e+30

def value_path_backward(value_gradient, input_arrays, adapter_product, value_weight, down_projected, up_projected):
    kv_cols = value_weight.shape[1] // N_TENSOR
    summed = jnp.zeros(input_arrays.shape, jnp.float32)
    backward_total = jnp.zeros((input_arrays.shape[0], down_projected.shape[1]), jnp.float32)
    for tensor_rank in range(N_TENSOR):
        first_col = tensor_rank * kv_cols
        grad_piece = value_gradient[:, first_col:first_col + kv_cols]
        lower_backward = jnp.dot(grad_piece, up_projected[:, first_col:first_col + kv_cols].T, preferred_element_type=jnp.float32).astype(jnp.bfloat16)
        partial_sum_term = jnp.dot(grad_piece, value_weight[:, first_col:first_col + kv_cols].T, preferred_element_type=jnp.float32)
        partial_sum_term = partial_sum_term + adapter_scale * jnp.dot(lower_backward, down_projected.T, preferred_element_type=jnp.float32)
        summed = summed + lax.optimization_barrier(partial_sum_term.astype(jnp.bfloat16)).astype(jnp.float32)
        backward_total = backward_total + lower_backward.astype(jnp.float32)
    up_factor_gradient = adapter_scale * jnp.dot(adapter_product.T, value_gradient, preferred_element_type=jnp.float32)
    down_factor_gradient = adapter_scale * jnp.dot(input_arrays.astype(jnp.float32).T, backward_total, precision=lax.Precision.HIGHEST)
    return (summed, down_factor_gradient, up_factor_gradient)

def reference(section_layer_input, value_projection_weight, adapter_down_weight, adapter_up_weight, output_weight, rotated_query_cache, rotated_key_cache, query_embedding, positives, hard_negative_passages, lengths):
    group = QH // KEY_VALUE_HEADS
    positions = jnp.arange(LEN, dtype=jnp.int32)
    is_valid = positions[None, :] < lengths[:, None]
    last_pick = (positions[None, :] == lengths[:, None] - 1).astype(jnp.float32)
    upper_input = section_layer_input[1]
    lower_upper_input = jnp.dot(upper_input, adapter_down_weight[1], preferred_element_type=jnp.float32).astype(jnp.bfloat16)
    upper_values = jnp.dot(upper_input, value_projection_weight[1], preferred_element_type=jnp.float32)
    upper_values = (upper_values + adapter_scale * jnp.dot(lower_upper_input, adapter_up_weight[1], preferred_element_type=jnp.float32)).astype(jnp.bfloat16)
    queries_top = rotated_query_cache[1].reshape(PASSAGES, LEN, KEY_VALUE_HEADS, group, HEAD_SIZE).astype(jnp.float32)
    last_query = jnp.einsum('pt,ptkgd->pkgd', last_pick, queries_top)
    keys_top = rotated_key_cache[1].reshape(PASSAGES, LEN, KEY_VALUE_HEADS, HEAD_SIZE).astype(jnp.float32)
    scores = jnp.einsum('pkgd,ptkd->pkgt', last_query, keys_top) / math.sqrt(HEAD_SIZE)
    scores = jnp.where(is_valid[:, None, None, :], scores, very_low)
    probs_top = jax.nn.softmax(scores, axis=-1).astype(jnp.bfloat16)
    values_grid = upper_values.reshape(PASSAGES, LEN, KEY_VALUE_HEADS, HEAD_SIZE).astype(jnp.float32)
    attended = jnp.einsum('pkgt,ptkd->pkgd', probs_top.astype(jnp.float32), values_grid).astype(jnp.bfloat16)
    attended = attended.reshape(PASSAGES, QH * HEAD_SIZE)
    mixed = jnp.dot(attended, output_weight[1], preferred_element_type=jnp.float32)
    last_in = jnp.einsum('pt,ptd->pd', last_pick, upper_input.reshape(PASSAGES, LEN, MODEL_WIDTH).astype(jnp.float32))
    pooled = last_in + mixed
    pooled_norm = jnp.sqrt(lax.optimization_barrier(jnp.sum(pooled * pooled, axis=-1, keepdims=True)) + tiny_eps)
    embedded = pooled / pooled_norm
    query_f = query_embedding.astype(jnp.float32)
    query_unit = query_f / jnp.sqrt(lax.optimization_barrier(jnp.sum(query_f * query_f, axis=-1, keepdims=True)) + tiny_eps)
    logits = jnp.dot(query_unit, embedded.T, precision=lax.Precision.HIGHEST) / tau_value
    passage_ids = jnp.arange(PASSAGES, dtype=jnp.int32)
    is_positive = jnp.any(positives[:, None] == passage_ids[None, :], axis=0)
    is_negative = jnp.any(hard_negative_passages[:, :, None] == passage_ids[None, None, :], axis=1)
    candidate = is_positive[None, :] | is_negative
    pos_hot = (positives[:, None] == passage_ids[None, :]).astype(jnp.float32)
    row_max = lax.optimization_barrier(jnp.max(jnp.where(candidate, logits, very_low), axis=-1))
    row_total = lax.optimization_barrier(jnp.sum(jnp.where(candidate, jnp.exp(logits - row_max[:, None]), 0.0), axis=-1))
    row_lse = row_max + jnp.log(row_total)
    query_loss = row_lse - lax.optimization_barrier(jnp.sum(pos_hot * logits, axis=-1))
    weights = jnp.where(candidate, jnp.exp(logits - row_lse[:, None]), 0.0) - pos_hot
    weights = weights * (loss_scale / (QUERIES * tau_value))
    grad_embed = jnp.dot(weights.T, query_unit, precision=lax.Precision.HIGHEST)
    along = lax.optimization_barrier(jnp.sum(embedded * grad_embed, axis=-1, keepdims=True))
    grad_pool = (grad_embed - embedded * along) / pooled_norm
    grad_att = jnp.dot(grad_pool.astype(jnp.bfloat16), output_weight[1].T, preferred_element_type=jnp.float32).astype(jnp.bfloat16)
    grad_att = grad_att.reshape(PASSAGES, KEY_VALUE_HEADS, group, HEAD_SIZE).astype(jnp.float32)
    upper_value_gradient = jnp.einsum('pkgt,pkgd->ptkd', probs_top.astype(jnp.float32), grad_att).astype(jnp.bfloat16)
    upper_value_gradient = upper_value_gradient.reshape(TOKENS, KEY_VALUE_HEADS * HEAD_SIZE)
    upper_partial_sum, upper_down_factor, upper_up_factor = value_path_backward(upper_value_gradient, upper_input, lower_upper_input, value_projection_weight[1], adapter_down_weight[1], adapter_up_weight[1])
    resid_top = jnp.einsum('pt,pd->ptd', last_pick, grad_pool).reshape(TOKENS, MODEL_WIDTH)
    grad_top = (upper_partial_sum + resid_top).astype(jnp.bfloat16)
    bottom_input = section_layer_input[0]
    lower_bottom_input = jnp.dot(bottom_input, adapter_down_weight[0], preferred_element_type=jnp.float32).astype(jnp.bfloat16)
    grad_att_low = jnp.dot(grad_top, output_weight[0].T, preferred_element_type=jnp.float32).astype(jnp.bfloat16)
    grad_att_low = grad_att_low.reshape(PASSAGES, LEN, KEY_VALUE_HEADS, group, HEAD_SIZE).astype(jnp.float32)
    queries_low = rotated_query_cache[0].reshape(PASSAGES, LEN, KEY_VALUE_HEADS, group, HEAD_SIZE).astype(jnp.float32)
    keys_low = rotated_key_cache[0].reshape(PASSAGES, LEN, KEY_VALUE_HEADS, HEAD_SIZE).astype(jnp.float32)
    scores_low = jnp.einsum('ptkgd,pukd->pkgtu', queries_low, keys_low) / math.sqrt(HEAD_SIZE)
    allowed = (positions[None, :, None] >= positions[None, None, :]) & is_valid[:, None, :]
    scores_low = jnp.where(allowed[:, None, None, :, :], scores_low, very_low)
    probs_low = jax.nn.softmax(scores_low, axis=-1).astype(jnp.bfloat16)
    lower_value_gradient = jnp.einsum('pkgtu,ptkgd->pukd', probs_low.astype(jnp.float32), grad_att_low).astype(jnp.bfloat16)
    lower_value_gradient = lower_value_gradient.reshape(TOKENS, KEY_VALUE_HEADS * HEAD_SIZE)
    lower_partial_sum, lower_down_factor, lower_up_factor = value_path_backward(lower_value_gradient, bottom_input, lower_bottom_input, value_projection_weight[0], adapter_down_weight[0], adapter_up_weight[0])
    grad_bottom = (lower_partial_sum + grad_top.astype(jnp.float32)).astype(jnp.bfloat16)
    return (query_loss, jnp.stack([grad_bottom, grad_top]), jnp.stack([lower_down_factor, upper_down_factor]), jnp.stack([lower_up_factor, upper_up_factor]))
```

```python
import functools
import math

import jax
import jax.numpy as jnp
from jax import lax
from jax.experimental import pallas as pl
from jax.experimental.pallas import tpu as pltpu
from jax.sharding import PartitionSpec as P

HEAD_SIZE = 128
KEY_VALUE_HEADS = 8
QH = 32

tau_value = 0.02
adapter_scale = 2.0
loss_scale = 65536.0
tiny_eps = 1e-06
very_low = -1e30
HIGH = lax.Precision.HIGHEST
F32 = jnp.float32
BF16 = jnp.bfloat16
MESH = pl.DeviceIdType.MESH


def round_up(value, unit):
    return (value + unit - 1) // unit * unit


def place(axes, sizes):
    me = 0
    for axis, size in zip(axes, sizes):
        me = me * size + lax.axis_index(axis)

    def coords(index):
        out = {}
        for axis, size in reversed(list(zip(axes, sizes))):
            out[axis] = lax.rem(index, size)
            index = lax.div(index, size)
        return out

    return me, coords


def enter(me, coords, n):
    barrier = pltpu.get_barrier_semaphore()

    @pl.loop(1, n)
    def _(k):
        pl.semaphore_signal(
            barrier, inc=1, device_id=coords(lax.rem(me + k, n)), device_id_type=MESH
        )

    pl.semaphore_wait(barrier, n - 1)


def push_all(me, coords, n, source, target, send_sem, recv_sem):
    def copy(k, to_index, slot):
        return pltpu.make_async_remote_copy(
            src_ref=source(to_index),
            dst_ref=target.at[slot],
            send_sem=send_sem.at[k],
            recv_sem=recv_sem.at[k],
            device_id=coords(to_index),
            device_id_type=MESH,
        )

    @pl.loop(1, n)
    def _(k):
        copy(k, lax.rem(me + k, n), me).start()

    @pl.loop(1, n)
    def _(k):
        copy(k, lax.rem(me + k, n), lax.rem(me + n - k, n)).wait()


def params(cid):
    return dict(
        compiler_params=pltpu.CompilerParams(
            collective_id=cid, has_side_effects=True, vmem_limit_bytes=40 * 1024 * 1024
        ),
        cost_estimate=pl.CostEstimate(
            flops=0, bytes_accessed=32 * 1024 * 1024, transcendentals=0
        ),
    )


def vmem(count):
    return [pl.BlockSpec(memory_space=pltpu.VMEM)] * count


def in_section(section, out_ref, run):
    if section is None:
        run()
        return
    here = lax.axis_index("section") == section
    pl.when(here)(run)

    @pl.when(jnp.logical_not(here))
    def _():
        out_ref[...] = jnp.zeros_like(out_ref)


def exchange_kernel(axes, sizes, same, section, x_ref, out_ref, send_sem, recv_sem):
    n = math.prod(sizes)

    def run():
        me, coords = place(axes, sizes)
        enter(me, coords, n)
        source = (lambda to: x_ref) if same else (lambda to: x_ref.at[to])
        out_ref[me] = x_ref[...] if same else x_ref[me]
        push_all(me, coords, n, source, out_ref, send_sem, recv_sem)

    in_section(section, out_ref, run)


def exchange(x, axes, cid, same=False, section=None):
    sizes = tuple(lax.axis_size(axis) for axis in axes)
    n = math.prod(sizes)
    shape = (n,) + x.shape if same else x.shape
    return pl.pallas_call(
        functools.partial(exchange_kernel, axes, sizes, same, section),
        out_shape=jax.ShapeDtypeStruct(shape, x.dtype),
        in_specs=vmem(1),
        out_specs=vmem(1)[0],
        scratch_shapes=[pltpu.SemaphoreType.DMA((n,)), pltpu.SemaphoreType.DMA((n,))],
        **params(cid),
    )(x)


def total_kernel(axes, sizes, section, x_ref, out_ref, held, send_a, recv_a, send_b, recv_b):
    n = math.prod(sizes)

    def run():
        me, coords = place(axes, sizes)
        enter(me, coords, n)
        held[me] = x_ref[me]
        push_all(me, coords, n, lambda to: x_ref.at[to], held, send_a, recv_a)
        out_ref[me] = jnp.sum(held[...].astype(F32), axis=0).astype(out_ref.dtype)
        push_all(me, coords, n, lambda to: out_ref.at[me], out_ref, send_b, recv_b)

    in_section(section, out_ref, run)


def total(arrays, axes, cid, section=None, dtype=F32):
    sizes = tuple(lax.axis_size(axis) for axis in axes)
    n = math.prod(sizes)
    flat = [a.reshape(-1).astype(dtype) for a in arrays]
    count = sum(a.size for a in flat)
    share = round_up(-(-count // n), 1024 if dtype == F32 else 2048)
    packed = jnp.concatenate(flat + [jnp.zeros((share * n - count,), dtype)])
    packed = packed.reshape(n, share // 128, 128)
    out = pl.pallas_call(
        functools.partial(total_kernel, axes, sizes, section),
        out_shape=jax.ShapeDtypeStruct(packed.shape, dtype),
        in_specs=vmem(1),
        out_specs=vmem(1)[0],
        scratch_shapes=[pltpu.VMEM(packed.shape, dtype)]
        + [pltpu.SemaphoreType.DMA((n,)) for _ in range(4)],
        **params(cid),
    )(packed).reshape(-1)
    results, at = [], 0
    for a in arrays:
        results.append(out[at : at + a.size].reshape(a.shape))
        at += a.size
    return results


def gather_kernel(n, x_ref, out_ref, send_a, recv_a, send_b, recv_b):
    half = n // 2

    def run():
        me, coords = place(("dp",), (n,))
        partner = me + 1 - 2 * lax.rem(me, 2)
        enter(me, coords, n)

        def along(k, to_index, slot):
            return pltpu.make_async_remote_copy(
                src_ref=x_ref,
                dst_ref=out_ref.at[slot],
                send_sem=send_a.at[k],
                recv_sem=recv_a.at[k],
                device_id=coords(to_index),
                device_id_type=MESH,
            )

        def across(k, source, slot):
            return pltpu.make_async_remote_copy(
                src_ref=source,
                dst_ref=out_ref.at[slot],
                send_sem=send_b.at[k],
                recv_sem=recv_b.at[k],
                device_id=coords(partner),
                device_id_type=MESH,
            )

        @pl.loop(1, half)
        def _(k):
            along(k, lax.rem(me + 2 * k, n), me).start()

        across(0, x_ref, me).start()
        out_ref[me] = x_ref[...]

        @pl.loop(1, half)
        def _(k):
            slot = lax.rem(me + n - 2 * k, n)
            along(k, lax.rem(me + 2 * k, n), slot).wait()
            across(k, out_ref.at[slot], slot).start()

        across(0, x_ref, partner).wait()

        @pl.loop(1, half)
        def _(k):
            slot = lax.rem(partner + n - 2 * k, n)
            across(k, out_ref.at[slot], slot).wait()

    in_section(0, out_ref, run)


def gather_low(x, cid):
    n = lax.axis_size("dp")
    return pl.pallas_call(
        functools.partial(gather_kernel, n),
        out_shape=jax.ShapeDtypeStruct((n,) + x.shape, x.dtype),
        in_specs=vmem(1),
        out_specs=vmem(1)[0],
        scratch_shapes=[pltpu.SemaphoreType.DMA((n,)) for _ in range(4)],
        **params(cid),
    )(x)


def relay_kernel(n, x_ref, out_ref, send_sem, recv_sem, down_sem):
    ti = lax.axis_index("tensor")
    section = lax.axis_index("section")
    barrier = pltpu.get_barrier_semaphore()
    pl.semaphore_signal(
        barrier, inc=1, device_id={"section": 1 - section}, device_id_type=MESH
    )

    @pl.loop(1, n)
    def _(k):
        pl.semaphore_signal(
            barrier, inc=1, device_id={"tensor": lax.rem(ti + k, n)}, device_id_type=MESH
        )

    pl.semaphore_wait(barrier, n)
    down = pltpu.make_async_remote_copy(
        src_ref=x_ref,
        dst_ref=out_ref.at[ti],
        send_sem=down_sem.at[0],
        recv_sem=down_sem.at[1],
        device_id={"section": 0},
        device_id_type=MESH,
    )
    coords = lambda index: {"tensor": index}

    @pl.when(section == 1)
    def _():
        down.start()
        out_ref[ti] = x_ref[...]
        push_all(ti, coords, n, lambda to: x_ref, out_ref, send_sem, recv_sem)
        down.wait_send()

    @pl.when(section == 0)
    def _():
        down.wait_recv()
        push_all(ti, coords, n, lambda to: out_ref.at[ti], out_ref, send_sem, recv_sem)


def relay(x, cid):
    n = lax.axis_size("tensor")
    return pl.pallas_call(
        functools.partial(relay_kernel, n),
        out_shape=jax.ShapeDtypeStruct((n,) + x.shape, x.dtype),
        in_specs=vmem(1),
        out_specs=vmem(1)[0],
        scratch_shapes=[pltpu.SemaphoreType.DMA((max(n, 2),)) for _ in range(3)],
        **params(cid),
    )(x)


def scatter_kernel(n, x_ref, out_ref, held, send_a, recv_a, down_sem):
    me, coords = place(("dp",), (n,))
    section = lax.axis_index("section")
    barrier = pltpu.get_barrier_semaphore()
    pl.semaphore_signal(
        barrier, inc=1, device_id={"section": 1 - section}, device_id_type=MESH
    )

    @pl.loop(1, n)
    def _(k):
        pl.semaphore_signal(
            barrier, inc=1, device_id=coords(lax.rem(me + k, n)), device_id_type=MESH
        )

    pl.semaphore_wait(barrier, n)
    held[me] = x_ref[me]
    push_all(me, coords, n, lambda to: x_ref.at[to], held, send_a, recv_a)
    out_ref[section] = jnp.sum(held[...].astype(F32), axis=0).astype(out_ref.dtype)
    down = pltpu.make_async_remote_copy(
        src_ref=out_ref.at[1],
        dst_ref=out_ref.at[1],
        send_sem=down_sem.at[0],
        recv_sem=down_sem.at[1],
        device_id={"section": 0},
        device_id_type=MESH,
    )

    @pl.when(section == 1)
    def _():
        out_ref[0] = jnp.zeros_like(out_ref[0])
        down.start()
        down.wait_send()

    @pl.when(section == 0)
    def _():
        down.wait_recv()


def scatter(x, cid):
    n = lax.axis_size("dp")
    return pl.pallas_call(
        functools.partial(scatter_kernel, n),
        out_shape=jax.ShapeDtypeStruct((2,) + x.shape[1:], x.dtype),
        in_specs=vmem(1),
        out_specs=vmem(1)[0],
        scratch_shapes=[pltpu.VMEM(x.shape, x.dtype)]
        + [pltpu.SemaphoreType.DMA((n,)) for _ in range(2)]
        + [pltpu.SemaphoreType.DMA((2,))],
        **params(cid),
    )(x)


def on_device(
    section_layer_input,
    value_projection_weight,
    adapter_down_weight,
    adapter_up_weight,
    output_weight,
    rotated_query_cache,
    rotated_key_cache,
    query_embedding,
    positives,
    hard_negative_passages,
    lengths,
):
    n_dp, n_tensor = lax.axis_size("dp"), lax.axis_size("tensor")
    is_top = lax.axis_index("section") == 1
    ti, di = lax.axis_index("tensor"), lax.axis_index("dp")
    x = section_layer_input[0]
    wv, down, up, wo = (
        value_projection_weight[0],
        adapter_down_weight[0],
        adapter_up_weight[0],
        output_weight[0],
    )
    rows, width = x.shape
    seqs = lengths.shape[0]
    toks = rows * n_tensor
    seq_len = toks // seqs
    cols = wv.shape[0]
    kv_cols = wv.shape[1]
    kv = kv_cols // HEAD_SIZE
    group = QH // KEY_VALUE_HEADS
    heads = kv * group
    rank = down.shape[1]
    own_q = query_embedding.shape[0]
    n_neg = hard_negative_passages.shape[1]
    n_q, n_p = n_dp * own_q, n_dp * seqs
    own_p = max(1, rows // seq_len)
    share = n_tensor * own_p // seqs
    own_first = ti * rows // seq_len

    down_cols = lax.dynamic_slice_in_dim(down, di * cols, cols, 0)
    wvf = (
        wv.astype(F32) + adapter_scale * jnp.dot(down_cols, up, preferred_element_type=F32)
    ).astype(BF16)
    wv_all = gather_low(wvf, 9).reshape(width, kv_cols)
    wv_heads = wvf.reshape(cols, kv, HEAD_SIZE)
    half_cols = wo.shape[0] // 2
    wo_below = lax.ppermute(wo[half_cols:], "section", [(0, 1)])

    positions = jnp.arange(seq_len, dtype=jnp.int32)
    is_valid = positions[None, :] < lengths[:, None]
    last_pick = (positions[None, :] == lengths[:, None] - 1).astype(BF16)
    query_grid = rotated_query_cache[0].reshape(seqs, seq_len, kv, group, HEAD_SIZE)
    key_grid = rotated_key_cache[0].reshape(seqs, seq_len, kv, HEAD_SIZE)
    last_query = jnp.einsum(
        "pt,pthd->phd",
        last_pick,
        rotated_query_cache[0].reshape(seqs, seq_len, heads, HEAD_SIZE),
        preferred_element_type=F32,
    ).astype(BF16)
    scores = jnp.einsum(
        "pkgd,ptkd->pkgt",
        last_query.reshape(seqs, kv, group, HEAD_SIZE),
        key_grid,
        preferred_element_type=F32,
    ) / math.sqrt(HEAD_SIZE)
    scores = jnp.where(is_valid[:, None, None, :], scores, very_low)
    probs_top = jax.nn.softmax(scores, axis=-1).astype(BF16)
    low = jnp.dot(x, down, preferred_element_type=F32).astype(BF16)
    probs_rows = probs_top.reshape(seqs * heads, seq_len)
    pad_rows = round_up(seqs * heads, 16)
    probs_rows = jnp.pad(probs_rows, ((0, pad_rows - seqs * heads), (0, 0)))
    probs_all = exchange(probs_rows, ("tensor",), 0, same=True)[:, : seqs * heads]
    probs_all = probs_all.reshape(n_tensor, seqs, heads, seq_len).transpose(1, 0, 2, 3)
    picks = jnp.concatenate(
        [probs_all.reshape(seqs, QH, seq_len), last_pick[:, None, :]], axis=1
    )
    picks_above = lax.ppermute(picks, "section", [(1, 0)])
    low_all = lax.all_gather(low, "tensor", axis=0, tiled=True)

    def fold():
        scores_low = jnp.einsum(
            "ptkgd,pukd->pkgtu", query_grid, key_grid, preferred_element_type=F32
        ) / math.sqrt(HEAD_SIZE)
        allowed = (positions[None, :, None] >= positions[None, None, :]) & is_valid[:, None, :]
        scores_low = jnp.where(allowed[:, None, None, :, :], scores_low, very_low)
        probs_low = jax.nn.softmax(scores_low, axis=-1).astype(BF16)
        return jnp.einsum(
            "pkgtu,pet->pkgue", probs_low, picks_above, preferred_element_type=F32
        ).astype(BF16)

    def bottom_fold():
        shape = (seqs, kv, group, seq_len, QH + 1)
        return lax.cond(is_top, lambda: jnp.zeros(shape, BF16), fold)

    def own_rows_of(full):
        part = lax.dynamic_slice_in_dim(full, own_first, own_p, 0)
        if share > 1:
            part = lax.dynamic_slice_in_dim(part, (ti % share) * rows, rows, 2)
        return part

    own_picks = own_rows_of(picks)
    picked = jnp.einsum(
        "pet,ptd->ped",
        own_picks,
        x.reshape(own_p, rows // own_p, width),
        preferred_element_type=F32,
    ).astype(BF16)
    by_block = picked.reshape(own_p, QH + 1, n_dp, cols).transpose(2, 0, 1, 3)
    head_part = by_block[:, :, :QH].reshape(n_dp, own_p, n_tensor, heads, cols)
    head_part = head_part.transpose(0, 2, 1, 3, 4).reshape(n_dp, n_tensor, own_p * heads, cols)
    last_part = by_block[:, :, QH]
    query_part = query_embedding.reshape(own_q, n_dp, cols).transpose(1, 0, 2)
    numbers = jnp.concatenate([positives[:, None], hard_negative_passages], axis=1)
    numbers = jnp.pad(numbers.astype(BF16), ((0, 0), (0, cols - 1 - n_neg)))
    numbers = jnp.broadcast_to(numbers[None], (n_dp, own_q, cols))
    tail = jnp.concatenate([last_part, query_part, numbers], axis=1)
    tail = jnp.broadcast_to(tail[:, None], (n_dp, n_tensor) + tail.shape[1:])
    message = jnp.concatenate([head_part, tail], axis=2)
    used = message.shape[2]
    message = jnp.pad(message, ((0, 0), (0, 0), (0, round_up(used, 16) - used), (0, 0)))
    got = exchange(message.reshape((n_dp * n_tensor,) + message.shape[2:]), ("dp", "tensor"), 1, section=1)
    got = got.reshape((n_dp, n_tensor) + got.shape[1:])
    first = own_p * heads

    def by_passage(part, count):
        part = part.reshape(n_dp, n_tensor // share, share, own_p, count, cols)
        if share > 1:
            part = jnp.sum(part.astype(F32), axis=2).astype(BF16)
        return part.reshape(n_p, count, cols)

    picked_all = by_passage(got[:, :, :first], heads).reshape(n_p, kv, group, cols)
    last_in = by_passage(got[:, :, first : first + own_p], 1)[:, 0].astype(F32)
    queries = got[:, 0, first + own_p : first + own_p + own_q].reshape(n_q, cols)
    numbers = got[:, 0, first + own_p + own_q : first + own_p + 2 * own_q].reshape(n_q, cols)
    all_pos = numbers[:, 0].astype(jnp.int32)
    all_neg = numbers[:, 1 : 1 + n_neg].astype(jnp.int32)

    attended = jnp.einsum("pkgd,dkc->pkgc", picked_all, wv_heads, preferred_element_type=F32)
    picked_low = jnp.einsum("pkgd,da->pkga", picked_all, down_cols, preferred_element_type=F32)
    attended, picked_low = total([attended, picked_low], ("dp",), 2, 1, BF16)
    attended = attended.reshape(n_p, heads * HEAD_SIZE).astype(BF16)
    mixed = jnp.dot(attended, wo, preferred_element_type=F32)
    mixed_rows = jnp.pad(mixed, ((0, round_up(n_p, 8) - n_p), (0, 0)))
    mixed = jnp.sum(exchange(mixed_rows, ("tensor",), 3, same=True, section=1), axis=0)[:n_p]
    pooled = last_in + mixed

    query_f = queries.astype(F32)
    pooled_hi = pooled.astype(BF16)
    pooled_lo = (pooled - pooled_hi.astype(F32)).astype(BF16)
    products = lax.dot_general(
        jnp.concatenate([queries, pooled_hi, pooled_lo], axis=0),
        wo,
        (((1,), (1,)), ((), ())),
        preferred_element_type=F32,
    )
    prod_q = products[:n_q]
    prod_p = products[n_q : n_q + n_p] + products[n_q + n_p :]
    dots = jnp.dot(query_f, pooled.T, precision=HIGH)
    prod_q, prod_p, dots, query_sq, pooled_sq = total(
        [prod_q, prod_p, dots, jnp.sum(query_f * query_f, -1), jnp.sum(pooled * pooled, -1)],
        ("dp",),
        4,
        1,
    )
    query_norm = jnp.sqrt(query_sq + tiny_eps)[:, None]
    pooled_norm = jnp.sqrt(pooled_sq + tiny_eps)[None, :]
    cosines = dots / query_norm / pooled_norm
    logits = cosines / tau_value
    passage_ids = jnp.arange(n_p, dtype=jnp.int32)
    pos_hot = (all_pos[:, None] == passage_ids[None, :]).astype(F32)
    is_positive = jnp.any(all_pos[:, None] == passage_ids[None, :], axis=0)
    is_negative = jnp.any(all_neg[:, :, None] == passage_ids[None, None, :], axis=1)
    candidate = is_positive[None, :] | is_negative
    row_max = jnp.max(jnp.where(candidate, logits, very_low), axis=-1)
    row_total = jnp.sum(jnp.where(candidate, jnp.exp(logits - row_max[:, None]), 0.0), axis=-1)
    row_lse = row_max + jnp.log(row_total)
    all_loss = row_lse - jnp.sum(pos_hot * logits, axis=-1)
    weights = jnp.where(candidate, jnp.exp(logits - row_lse[:, None]), 0.0) - pos_hot
    weights = weights * (loss_scale / (n_q * tau_value))
    along = jnp.sum(weights * cosines, axis=0)
    norm = pooled_norm[0][:, None]
    coef_q = (weights / query_norm).T / norm
    coef_p = along[:, None] / (norm * norm)
    grad_pool = (jnp.dot(coef_q, query_f, precision=HIGH) - coef_p * pooled).astype(BF16)
    grad_att = (jnp.dot(coef_q, prod_q, precision=HIGH) - coef_p * prod_p).astype(BF16)

    grad_heads = grad_att.reshape(n_p, kv, group, HEAD_SIZE)
    pulled = jnp.einsum("pkgc,dkc->pkgd", grad_heads, wv_heads, preferred_element_type=F32)
    pulled = pulled.astype(BF16).reshape(n_p, heads, cols)
    to_send = jnp.concatenate([pulled.reshape(n_p * heads, cols), grad_pool], axis=0)
    to_send = jnp.pad(to_send, ((0, round_up(to_send.shape[0], 16) - to_send.shape[0]), (0, 0)))
    folded = bottom_fold()
    to_send, folded, wv_all = lax.optimization_barrier((to_send, folded, wv_all))
    from_group = relay(to_send, 5)

    above_heads = from_group[:, : n_p * heads].reshape(n_tensor, n_p, heads, cols)
    above_heads = above_heads.transpose(1, 0, 2, 3).reshape(n_p, QH, cols)
    above_pool = from_group[0, n_p * heads : n_p * heads + n_p]
    above_rows = jnp.concatenate([above_heads, above_pool[:, None, :]], axis=1)
    spread = lax.dot_general(
        above_rows.reshape(n_p * (QH + 1), cols),
        jnp.where(is_top, wo_below, wo[:half_cols]),
        (((1,), (1,)), ((), ())),
        preferred_element_type=F32,
    ).astype(BF16)
    spread = spread.reshape(n_dp, -1, 128)
    used = spread.shape[1]
    spread = jnp.pad(spread, ((0, 0), (0, round_up(used, 16) - used), (0, 0)))
    spread = scatter(spread, 10)[:, :used].reshape(2, seqs * (QH + 1), half_cols)
    spread = jnp.concatenate([spread[0], spread[1]], axis=1)
    spread = spread.reshape(seqs, QH + 1, kv, group, HEAD_SIZE)

    pulled = jnp.concatenate([pulled, grad_pool[:, None, :]], axis=1)
    pulled = pulled.reshape(n_dp, n_tensor // share, own_p * (heads + 1), cols)
    used = own_p * (heads + 1)
    pulled = jnp.pad(pulled, ((0, 0), (0, 0), (0, round_up(used, 16) - used), (0, 0)))
    pulled = jnp.repeat(pulled, share, axis=1)
    own_pulled = exchange(
        pulled.reshape((n_dp * n_tensor,) + pulled.shape[2:]), ("dp", "tensor"), 6, section=1
    )[:, :used]
    own_pulled = own_pulled.reshape(n_dp, n_tensor, own_p, heads + 1, cols)
    pulled_heads = own_pulled[:, :, :, :heads].transpose(2, 1, 3, 0, 4).reshape(own_p, QH, width)
    pulled_last = own_pulled[:, 0, :, heads].transpose(1, 0, 2).reshape(own_p, 1, width)
    pulled_rows = jnp.concatenate([pulled_heads, pulled_last], axis=1)
    pulled_below = lax.ppermute(pulled_rows, "section", [(1, 0)])
    own_above = own_rows_of(picks_above)
    grad_top = jnp.einsum(
        "pet,ped->ptd",
        jnp.where(is_top, own_picks, own_above),
        jnp.where(is_top, pulled_rows, pulled_below),
        preferred_element_type=F32,
    )
    grad_top = grad_top.astype(BF16).reshape(rows, width)
    up_heads = up.reshape(rank, kv, HEAD_SIZE)
    up_top = adapter_scale * jnp.einsum(
        "pkga,pkgc->akc", picked_low.astype(BF16), grad_heads, preferred_element_type=F32
    ).reshape(rank, kv_cols)
    back_top = jnp.einsum(
        "pkgc,akc->pkga", grad_heads, up_heads, preferred_element_type=F32
    ).astype(BF16)
    down_top = adapter_scale * jnp.einsum(
        "pkga,pkgd->ad", back_top, picked_all, preferred_element_type=F32
    )

    grad_values = jnp.einsum(
        "pkgue,pekgc->pukc", folded, spread, preferred_element_type=F32
    ).astype(BF16)
    grad_values = grad_values.reshape(toks, kv_cols)
    term = lax.dot_general(
        grad_values, wv_all, (((1,), (1,)), ((), ())), preferred_element_type=F32
    ).astype(BF16)
    back = lax.dot_general(
        grad_values, up, (((1,), (1,)), ((), ())), preferred_element_type=F32
    ).astype(BF16)
    parts = exchange(
        jnp.concatenate([term, jnp.pad(back, ((0, 0), (0, 128 - rank)))], axis=1).reshape(
            n_tensor, rows, width + 128
        ),
        ("tensor",),
        7,
        section=0,
    )
    parts = jnp.sum(parts.astype(F32), axis=0)
    grad_bottom = (parts[:, :width] + grad_top.astype(F32)).astype(BF16)
    back_own = parts[:, width : width + rank].astype(BF16)
    down_low = adapter_scale * lax.dot_general(
        back_own, x, (((0,), (0,)), ((), ())), preferred_element_type=F32
    )
    up_low = adapter_scale * lax.dot_general(
        low_all, grad_values, (((0,), (0,)), ((), ())), preferred_element_type=F32
    )

    grad_input = jnp.where(is_top, grad_top, grad_bottom)
    down_top = lax.dynamic_update_slice_in_dim(
        jnp.zeros((rank, width), F32), down_top, di * cols, 1
    )
    grad_down = jnp.where(is_top, down_top, down_low)
    grad_up = jnp.where(is_top, jnp.where(di == 0, up_top, 0.0), up_low)
    ups = lax.dynamic_update_slice_in_dim(
        jnp.zeros((n_tensor, rank, kv_cols), F32), grad_up[None], ti, 0
    )
    grad_down, ups = total([grad_down, ups], ("dp", "tensor"), 8, None, BF16)
    grad_down, ups = grad_down.T.astype(F32), ups.astype(F32)
    grad_up = lax.dynamic_slice_in_dim(ups, ti, 1, 0)
    own_loss = lax.dynamic_slice_in_dim(all_loss, di * own_q, own_q, 0)
    below_loss = lax.ppermute(own_loss, "section", [(1, 0)])
    query_loss = jnp.where(is_top, own_loss, below_loss)
    return (query_loss, grad_input[None], grad_down[None], grad_up)


def solution(mesh):
    return jax.shard_map(
        on_device,
        mesh=mesh,
        in_specs=(
            P("section", ("dp", "tensor"), None),
            P("section", "dp", "tensor"),
            P("section", None, None),
            P("section", None, "tensor"),
            P("section", "tensor", "dp"),
            P("section", "dp", "tensor"),
            P("section", "dp", "tensor"),
            P("dp", None),
            P("dp"),
            P("dp", None),
            P("dp"),
        ),
        out_specs=(
            P("dp"),
            P("section", ("dp", "tensor"), None),
            P("section", None, None),
            P("section", None, "tensor"),
        ),
        check_vma=False,
    )
```

```python
import functools
import math

import jax
import jax.numpy as jnp
from jax import lax
from jax.experimental import pallas as pl
from jax.experimental.pallas import tpu as pltpu
from jax.sharding import PartitionSpec as P

HEAD_SIZE = 128
KEY_VALUE_HEADS = 8
QH = 32

tau_value = 0.02
adapter_scale = 2.0
loss_scale = 65536.0
tiny_eps = 1e-06
very_low = -1e30
HIGH = lax.Precision.HIGHEST
F32 = jnp.float32
BF16 = jnp.bfloat16
MESH = pl.DeviceIdType.MESH


def round_up(value, unit):
    return (value + unit - 1) // unit * unit


def place(axes, sizes):
    me = 0
    for axis, size in zip(axes, sizes):
        me = me * size + lax.axis_index(axis)

    def coords(index):
        out = {}
        for axis, size in reversed(list(zip(axes, sizes))):
            out[axis] = lax.rem(index, size)
            index = lax.div(index, size)
        return out

    return me, coords


def each_peer(n):
    def run(body):
        if n <= 16:
            for k in range(1, n):
                body(k)
        else:
            pl.loop(1, n)(body)

    return run


def enter(me, coords, n):
    barrier = pltpu.get_barrier_semaphore()

    @each_peer(n)
    def _(k):
        pl.semaphore_signal(
            barrier, inc=1, device_id=coords(lax.rem(me + k, n)), device_id_type=MESH
        )

    pl.semaphore_wait(barrier, n - 1)


def push_all(me, coords, n, source, target, send_sem, recv_sem):
    def copy(k, to_index, slot):
        return pltpu.make_async_remote_copy(
            src_ref=source(to_index),
            dst_ref=target.at[slot],
            send_sem=send_sem.at[k],
            recv_sem=recv_sem.at[k],
            device_id=coords(to_index),
            device_id_type=MESH,
        )

    @each_peer(n)
    def _(k):
        copy(k, lax.rem(me + k, n), me).start()

    @each_peer(n)
    def _(k):
        copy(k, lax.rem(me + k, n), lax.rem(me + n - k, n)).wait()


def params(cid):
    return dict(
        compiler_params=pltpu.CompilerParams(
            collective_id=cid, has_side_effects=True, vmem_limit_bytes=40 * 1024 * 1024
        ),
        cost_estimate=pl.CostEstimate(
            flops=0, bytes_accessed=32 * 1024 * 1024, transcendentals=0
        ),
    )


def vmem(count):
    return [pl.BlockSpec(memory_space=pltpu.VMEM)] * count


def in_section(section, out_ref, run):
    if section is None:
        run()
        return
    here = lax.axis_index("section") == section
    pl.when(here)(run)

    @pl.when(jnp.logical_not(here))
    def _():
        out_ref[...] = jnp.zeros_like(out_ref)


def exchange_kernel(axes, sizes, same, section, x_ref, out_ref, send_sem, recv_sem):
    n = math.prod(sizes)

    def run():
        me, coords = place(axes, sizes)
        enter(me, coords, n)
        source = (lambda to: x_ref) if same else (lambda to: x_ref.at[to])
        out_ref[me] = x_ref[...] if same else x_ref[me]
        push_all(me, coords, n, source, out_ref, send_sem, recv_sem)

    in_section(section, out_ref, run)


def exchange(x, axes, cid, same=False, section=None):
    sizes = tuple(lax.axis_size(axis) for axis in axes)
    n = math.prod(sizes)
    shape = (n,) + x.shape if same else x.shape
    return pl.pallas_call(
        functools.partial(exchange_kernel, axes, sizes, same, section),
        out_shape=jax.ShapeDtypeStruct(shape, x.dtype),
        in_specs=vmem(1),
        out_specs=vmem(1)[0],
        scratch_shapes=[pltpu.SemaphoreType.DMA((n,)), pltpu.SemaphoreType.DMA((n,))],
        **params(cid),
    )(x)


def total_kernel(axes, sizes, section, x_ref, out_ref, held, send_a, recv_a, send_b, recv_b):
    n = math.prod(sizes)

    def run():
        me, coords = place(axes, sizes)
        enter(me, coords, n)
        held[me] = x_ref[me]
        push_all(me, coords, n, lambda to: x_ref.at[to], held, send_a, recv_a)
        out_ref[me] = jnp.sum(held[...].astype(F32), axis=0).astype(out_ref.dtype)
        push_all(me, coords, n, lambda to: out_ref.at[me], out_ref, send_b, recv_b)

    in_section(section, out_ref, run)


def total(arrays, axes, cid, section=None, dtype=F32):
    sizes = tuple(lax.axis_size(axis) for axis in axes)
    n = math.prod(sizes)
    flat = [a.reshape(-1).astype(dtype) for a in arrays]
    count = sum(a.size for a in flat)
    share = round_up(-(-count // n), 1024 if dtype == F32 else 2048)
    packed = jnp.concatenate(flat + [jnp.zeros((share * n - count,), dtype)])
    packed = packed.reshape(n, share // 128, 128)
    out = pl.pallas_call(
        functools.partial(total_kernel, axes, sizes, section),
        out_shape=jax.ShapeDtypeStruct(packed.shape, dtype),
        in_specs=vmem(1),
        out_specs=vmem(1)[0],
        scratch_shapes=[pltpu.VMEM(packed.shape, dtype)]
        + [pltpu.SemaphoreType.DMA((n,)) for _ in range(4)],
        **params(cid),
    )(packed).reshape(-1)
    results, at = [], 0
    for a in arrays:
        results.append(out[at : at + a.size].reshape(a.shape))
        at += a.size
    return results


def opening_kernel(
    sizes,
    x_ref,
    wv_ref,
    wo_ref,
    picks_ref,
    got_ref,
    all_ref,
    below_ref,
    above_ref,
    send_sem,
    recv_sem,
    send_a,
    recv_a,
    send_b,
    recv_b,
    cross,
):
    n, n_dp = math.prod(sizes), sizes[0]
    half = n_dp // 2
    section = lax.axis_index("section")
    me, coords = place(("dp", "tensor"), sizes)
    barrier = pltpu.get_barrier_semaphore()
    pl.semaphore_signal(
        barrier, inc=1, device_id={"section": 1 - section}, device_id_type=MESH
    )

    @each_peer(n)
    def _(k):
        pl.semaphore_signal(
            barrier, inc=1, device_id=coords(lax.rem(me + k, n)), device_id_type=MESH
        )

    pl.semaphore_wait(barrier, n)

    def crossing(source, target, first, to):
        return pltpu.make_async_remote_copy(
            src_ref=source,
            dst_ref=target,
            send_sem=cross.at[first],
            recv_sem=cross.at[first + 1],
            device_id={"section": to},
            device_id_type=MESH,
        )

    rows = below_ref.shape[0]
    picks_down = crossing(picks_ref, above_ref, 0, 0)
    weight_up = crossing(wo_ref.at[pl.ds(rows, rows)], below_ref, 2, 1)

    @pl.when(section == 1)
    def _():
        picks_down.start()
        got_ref[me] = x_ref[me]
        push_all(me, coords, n, lambda to: x_ref.at[to], got_ref, send_sem, recv_sem)
        picks_down.wait_send()
        weight_up.wait_recv()

    @pl.when(section == 0)
    def _():
        weight_up.start()
        di = lax.axis_index("dp")
        partner = di + 1 - 2 * lax.rem(di, 2)

        def along(k, to_index, slot):
            return pltpu.make_async_remote_copy(
                src_ref=wv_ref,
                dst_ref=all_ref.at[slot],
                send_sem=send_a.at[k],
                recv_sem=recv_a.at[k],
                device_id={"dp": to_index},
                device_id_type=MESH,
            )

        def across(k, source, slot):
            return pltpu.make_async_remote_copy(
                src_ref=source,
                dst_ref=all_ref.at[slot],
                send_sem=send_b.at[k],
                recv_sem=recv_b.at[k],
                device_id={"dp": partner},
                device_id_type=MESH,
            )

        @each_peer(half)
        def _(k):
            along(k, lax.rem(di + 2 * k, n_dp), di).start()

        across(0, wv_ref, di).start()
        all_ref[di] = wv_ref[...]
        got_ref[...] = jnp.zeros_like(got_ref)

        @each_peer(half)
        def _(k):
            slot = lax.rem(di + n_dp - 2 * k, n_dp)
            along(k, lax.rem(di + 2 * k, n_dp), slot).wait()
            across(k, all_ref.at[slot], slot).start()

        across(0, wv_ref, partner).wait()

        @each_peer(half)
        def _(k):
            slot = lax.rem(partner + n_dp - 2 * k, n_dp)
            across(k, all_ref.at[slot], slot).wait()

        weight_up.wait_send()
        picks_down.wait_recv()


def opening(x, wv, wo, picks, cid):
    sizes = (lax.axis_size("dp"), lax.axis_size("tensor"))
    n, n_dp = math.prod(sizes), sizes[0]
    shape = jax.ShapeDtypeStruct
    hbm = pl.BlockSpec(memory_space=pl.ANY)
    return pl.pallas_call(
        functools.partial(opening_kernel, sizes),
        out_shape=(
            shape(x.shape, x.dtype),
            shape((n_dp,) + wv.shape, wv.dtype),
            shape((wo.shape[0] // 2, wo.shape[1]), wo.dtype),
            shape(picks.shape, picks.dtype),
        ),
        in_specs=vmem(2) + [hbm] + vmem(1),
        out_specs=tuple(vmem(2) + [hbm] + vmem(1)),
        scratch_shapes=[pltpu.SemaphoreType.DMA((n,)) for _ in range(2)]
        + [pltpu.SemaphoreType.DMA((n_dp,)) for _ in range(4)]
        + [pltpu.SemaphoreType.DMA((4,))],
        **params(cid),
    )(x, wv, wo, picks)


def relay_kernel(n, x_ref, out_ref, send_sem, recv_sem, down_sem):
    ti = lax.axis_index("tensor")
    section = lax.axis_index("section")
    barrier = pltpu.get_barrier_semaphore()
    pl.semaphore_signal(
        barrier, inc=1, device_id={"section": 1 - section}, device_id_type=MESH
    )

    @each_peer(n)
    def _(k):
        pl.semaphore_signal(
            barrier, inc=1, device_id={"tensor": lax.rem(ti + k, n)}, device_id_type=MESH
        )

    pl.semaphore_wait(barrier, n)
    down = pltpu.make_async_remote_copy(
        src_ref=x_ref,
        dst_ref=out_ref.at[ti],
        send_sem=down_sem.at[0],
        recv_sem=down_sem.at[1],
        device_id={"section": 0},
        device_id_type=MESH,
    )
    coords = lambda index: {"tensor": index}

    @pl.when(section == 1)
    def _():
        down.start()
        out_ref[ti] = x_ref[...]
        push_all(ti, coords, n, lambda to: x_ref, out_ref, send_sem, recv_sem)
        down.wait_send()

    @pl.when(section == 0)
    def _():
        down.wait_recv()
        push_all(ti, coords, n, lambda to: out_ref.at[ti], out_ref, send_sem, recv_sem)


def relay(x, cid):
    n = lax.axis_size("tensor")
    return pl.pallas_call(
        functools.partial(relay_kernel, n),
        out_shape=jax.ShapeDtypeStruct((n,) + x.shape, x.dtype),
        in_specs=vmem(1),
        out_specs=vmem(1)[0],
        scratch_shapes=[pltpu.SemaphoreType.DMA((max(n, 2),)) for _ in range(3)],
        **params(cid),
    )(x)


def scatter_kernel(n, x_ref, out_ref, held, send_a, recv_a, down_sem):
    me, coords = place(("dp",), (n,))
    section = lax.axis_index("section")
    barrier = pltpu.get_barrier_semaphore()
    pl.semaphore_signal(
        barrier, inc=1, device_id={"section": 1 - section}, device_id_type=MESH
    )

    @each_peer(n)
    def _(k):
        pl.semaphore_signal(
            barrier, inc=1, device_id=coords(lax.rem(me + k, n)), device_id_type=MESH
        )

    pl.semaphore_wait(barrier, n)
    held[me] = x_ref[me]
    push_all(me, coords, n, lambda to: x_ref.at[to], held, send_a, recv_a)
    out_ref[section] = jnp.sum(held[...].astype(F32), axis=0).astype(out_ref.dtype)
    down = pltpu.make_async_remote_copy(
        src_ref=out_ref.at[1],
        dst_ref=out_ref.at[1],
        send_sem=down_sem.at[0],
        recv_sem=down_sem.at[1],
        device_id={"section": 0},
        device_id_type=MESH,
    )

    @pl.when(section == 1)
    def _():
        out_ref[0] = jnp.zeros_like(out_ref[0])
        down.start()
        down.wait_send()

    @pl.when(section == 0)
    def _():
        down.wait_recv()


def scatter(x, cid):
    n = lax.axis_size("dp")
    return pl.pallas_call(
        functools.partial(scatter_kernel, n),
        out_shape=jax.ShapeDtypeStruct((2,) + x.shape[1:], x.dtype),
        in_specs=vmem(1),
        out_specs=vmem(1)[0],
        scratch_shapes=[pltpu.VMEM(x.shape, x.dtype)]
        + [pltpu.SemaphoreType.DMA((n,)) for _ in range(2)]
        + [pltpu.SemaphoreType.DMA((2,))],
        **params(cid),
    )(x)


def on_device(
    section_layer_input,
    value_projection_weight,
    adapter_down_weight,
    adapter_up_weight,
    output_weight,
    rotated_query_cache,
    rotated_key_cache,
    query_embedding,
    positives,
    hard_negative_passages,
    lengths,
):
    n_dp, n_tensor = lax.axis_size("dp"), lax.axis_size("tensor")
    is_top = lax.axis_index("section") == 1
    ti, di = lax.axis_index("tensor"), lax.axis_index("dp")
    x = section_layer_input[0]
    wv, down, up, wo = (
        value_projection_weight[0],
        adapter_down_weight[0],
        adapter_up_weight[0],
        output_weight[0],
    )
    rows, width = x.shape
    seqs = lengths.shape[0]
    toks = rows * n_tensor
    seq_len = toks // seqs
    cols = wv.shape[0]
    kv_cols = wv.shape[1]
    kv = kv_cols // HEAD_SIZE
    group = QH // KEY_VALUE_HEADS
    heads = kv * group
    rank = down.shape[1]
    own_q = query_embedding.shape[0]
    n_neg = hard_negative_passages.shape[1]
    n_q, n_p = n_dp * own_q, n_dp * seqs
    own_p = max(1, rows // seq_len)
    share = n_tensor * own_p // seqs
    own_first = ti * rows // seq_len

    down_cols = lax.dynamic_slice_in_dim(down, di * cols, cols, 0)
    wvf = (
        wv.astype(F32) + adapter_scale * jnp.dot(down_cols, up, preferred_element_type=F32)
    ).astype(BF16)
    wv_heads = wvf.reshape(cols, kv, HEAD_SIZE)
    half_cols = wo.shape[0] // 2

    positions = jnp.arange(seq_len, dtype=jnp.int32)
    is_valid = positions[None, :] < lengths[:, None]
    last_pick = (positions[None, :] == lengths[:, None] - 1).astype(BF16)
    query_grid = rotated_query_cache[0].reshape(seqs, seq_len, kv, group, HEAD_SIZE)
    key_grid = rotated_key_cache[0].reshape(seqs, seq_len, kv, HEAD_SIZE)
    last_query = jnp.einsum(
        "pt,pthd->phd",
        last_pick,
        rotated_query_cache[0].reshape(seqs, seq_len, heads, HEAD_SIZE),
        preferred_element_type=F32,
    ).astype(BF16)
    scores = jnp.einsum(
        "pkgd,ptkd->pkgt",
        last_query.reshape(seqs, kv, group, HEAD_SIZE),
        key_grid,
        preferred_element_type=F32,
    ) / math.sqrt(HEAD_SIZE)
    scores = jnp.where(is_valid[:, None, None, :], scores, very_low)
    probs_top = jax.nn.softmax(scores, axis=-1).astype(BF16)
    low = jnp.dot(x, down, preferred_element_type=F32).astype(BF16)
    probs_rows = probs_top.reshape(seqs * heads, seq_len)
    pad_rows = round_up(seqs * heads, 16)
    probs_rows = jnp.pad(probs_rows, ((0, pad_rows - seqs * heads), (0, 0)))
    low_rows = jnp.pad(low, ((0, 0), (0, seq_len - rank)))
    probs_all = exchange(
        jnp.concatenate([probs_rows, low_rows], axis=0), ("tensor",), 0, same=True
    )
    low_all = probs_all[:, pad_rows : pad_rows + rows, :rank].reshape(toks, rank)
    probs_all = probs_all[:, : seqs * heads]
    probs_all = probs_all.reshape(n_tensor, seqs, heads, seq_len).transpose(1, 0, 2, 3)
    picks = jnp.concatenate(
        [probs_all.reshape(seqs, QH, seq_len), last_pick[:, None, :]], axis=1
    )

    def fold():
        scores_low = jnp.einsum(
            "ptkgd,pukd->pkgtu", query_grid, key_grid, preferred_element_type=F32
        ) / math.sqrt(HEAD_SIZE)
        allowed = (positions[None, :, None] >= positions[None, None, :]) & is_valid[:, None, :]
        scores_low = jnp.where(allowed[:, None, None, :, :], scores_low, very_low)
        probs_low = jax.nn.softmax(scores_low, axis=-1).astype(BF16)
        return jnp.einsum(
            "pkgtu,pet->pkgue", probs_low, picks_above, preferred_element_type=F32
        ).astype(BF16)

    def bottom_fold():
        shape = (seqs, kv, group, seq_len, QH + 1)
        return lax.cond(is_top, lambda: jnp.zeros(shape, BF16), fold)

    def own_rows_of(full):
        part = lax.dynamic_slice_in_dim(full, own_first, own_p, 0)
        if share > 1:
            part = lax.dynamic_slice_in_dim(part, (ti % share) * rows, rows, 2)
        return part

    own_picks = own_rows_of(picks)
    picked = jnp.einsum(
        "pet,ptd->ped",
        own_picks,
        x.reshape(own_p, rows // own_p, width),
        preferred_element_type=F32,
    ).astype(BF16)
    by_block = picked.reshape(own_p, QH + 1, n_dp, cols).transpose(2, 0, 1, 3)
    head_part = by_block[:, :, :QH].reshape(n_dp, own_p, n_tensor, heads, cols)
    head_part = head_part.transpose(0, 2, 1, 3, 4).reshape(n_dp, n_tensor, own_p * heads, cols)
    last_part = by_block[:, :, QH]
    query_part = query_embedding.reshape(own_q, n_dp, cols).transpose(1, 0, 2)
    numbers = jnp.concatenate([positives[:, None], hard_negative_passages], axis=1)
    numbers = jnp.pad(numbers.astype(BF16), ((0, 0), (0, cols - 1 - n_neg)))
    numbers = jnp.broadcast_to(numbers[None], (n_dp, own_q, cols))
    tail = jnp.concatenate([last_part, query_part, numbers], axis=1)
    tail = jnp.broadcast_to(tail[:, None], (n_dp, n_tensor) + tail.shape[1:])
    message = jnp.concatenate([head_part, tail], axis=2)
    used = message.shape[2]
    message = jnp.pad(message, ((0, 0), (0, 0), (0, round_up(used, 16) - used), (0, 0)))
    pad_picks = jnp.pad(picks, ((0, 0), (0, round_up(QH + 1, 16) - QH - 1), (0, 0)))
    got, wv_all, wo_below, picks_above = opening(
        message.reshape((n_dp * n_tensor,) + message.shape[2:]), wvf, wo, pad_picks, 1
    )
    wv_all = wv_all.reshape(width, kv_cols)
    picks_above = picks_above[:, : QH + 1]
    got = got.reshape((n_dp, n_tensor) + got.shape[1:])
    first = own_p * heads

    def by_passage(part, count):
        part = part.reshape(n_dp, n_tensor // share, share, own_p, count, cols)
        if share > 1:
            part = jnp.sum(part.astype(F32), axis=2).astype(BF16)
        return part.reshape(n_p, count, cols)

    picked_all = by_passage(got[:, :, :first], heads).reshape(n_p, kv, group, cols)
    last_in = by_passage(got[:, :, first : first + own_p], 1)[:, 0].astype(F32)
    queries = got[:, 0, first + own_p : first + own_p + own_q].reshape(n_q, cols)
    numbers = got[:, 0, first + own_p + own_q : first + own_p + 2 * own_q].reshape(n_q, cols)
    all_pos = numbers[:, 0].astype(jnp.int32)
    all_neg = numbers[:, 1 : 1 + n_neg].astype(jnp.int32)

    attended = jnp.einsum("pkgd,dkc->pkgc", picked_all, wv_heads, preferred_element_type=F32)
    picked_low = jnp.einsum("pkgd,da->pkga", picked_all, down_cols, preferred_element_type=F32)
    attended, picked_low = total([attended, picked_low], ("dp",), 2, 1, BF16)
    attended = attended.reshape(n_p, heads * HEAD_SIZE).astype(BF16)
    mixed = jnp.dot(attended, wo, preferred_element_type=F32)
    mixed_rows = jnp.pad(mixed, ((0, round_up(n_p, 8) - n_p), (0, 0)))
    mixed = jnp.sum(exchange(mixed_rows, ("tensor",), 3, same=True, section=1), axis=0)[:n_p]
    pooled = last_in + mixed

    query_f = queries.astype(F32)
    pooled_hi = pooled.astype(BF16)
    pooled_lo = (pooled - pooled_hi.astype(F32)).astype(BF16)
    products = lax.dot_general(
        jnp.concatenate([queries, pooled_hi, pooled_lo], axis=0),
        wo,
        (((1,), (1,)), ((), ())),
        preferred_element_type=F32,
    )
    prod_q = products[:n_q]
    prod_p = products[n_q : n_q + n_p] + products[n_q + n_p :]
    dots = jnp.dot(query_f, pooled.T, precision=HIGH)
    prod_q, prod_p, dots, query_sq, pooled_sq = total(
        [prod_q, prod_p, dots, jnp.sum(query_f * query_f, -1), jnp.sum(pooled * pooled, -1)],
        ("dp",),
        4,
        1,
    )
    query_norm = jnp.sqrt(query_sq + tiny_eps)[:, None]
    pooled_norm = jnp.sqrt(pooled_sq + tiny_eps)[None, :]
    cosines = dots / query_norm / pooled_norm
    logits = cosines / tau_value
    passage_ids = jnp.arange(n_p, dtype=jnp.int32)
    pos_hot = (all_pos[:, None] == passage_ids[None, :]).astype(F32)
    is_positive = jnp.any(all_pos[:, None] == passage_ids[None, :], axis=0)
    is_negative = jnp.any(all_neg[:, :, None] == passage_ids[None, None, :], axis=1)
    candidate = is_positive[None, :] | is_negative
    row_max = jnp.max(jnp.where(candidate, logits, very_low), axis=-1)
    row_total = jnp.sum(jnp.where(candidate, jnp.exp(logits - row_max[:, None]), 0.0), axis=-1)
    row_lse = row_max + jnp.log(row_total)
    all_loss = row_lse - jnp.sum(pos_hot * logits, axis=-1)
    weights = jnp.where(candidate, jnp.exp(logits - row_lse[:, None]), 0.0) - pos_hot
    weights = weights * (loss_scale / (n_q * tau_value))
    along = jnp.sum(weights * cosines, axis=0)
    norm = pooled_norm[0][:, None]
    coef_q = (weights / query_norm).T / norm
    coef_p = along[:, None] / (norm * norm)
    grad_pool = (jnp.dot(coef_q, query_f, precision=HIGH) - coef_p * pooled).astype(BF16)
    grad_att = (jnp.dot(coef_q, prod_q, precision=HIGH) - coef_p * prod_p).astype(BF16)

    grad_heads = grad_att.reshape(n_p, kv, group, HEAD_SIZE)
    pulled = jnp.einsum("pkgc,dkc->pkgd", grad_heads, wv_heads, preferred_element_type=F32)
    pulled = pulled.astype(BF16).reshape(n_p, heads, cols)
    to_send = jnp.concatenate([pulled.reshape(n_p * heads, cols), grad_pool], axis=0)
    to_send = jnp.pad(to_send, ((0, round_up(to_send.shape[0], 16) - to_send.shape[0]), (0, 0)))
    pulled = jnp.concatenate([pulled, grad_pool[:, None, :]], axis=1)
    pulled = pulled.reshape(n_dp, n_tensor // share, own_p * (heads + 1), cols)
    used = own_p * (heads + 1)
    pulled = jnp.pad(pulled, ((0, 0), (0, 0), (0, round_up(used, 16) - used), (0, 0)))
    pulled = jnp.repeat(pulled, share, axis=1)
    own_pulled = exchange(
        pulled.reshape((n_dp * n_tensor,) + pulled.shape[2:]), ("dp", "tensor"), 6, section=1
    )[:, :used]
    own_pulled = own_pulled.reshape(n_dp, n_tensor, own_p, heads + 1, cols)
    pulled_heads = own_pulled[:, :, :, :heads].transpose(2, 1, 3, 0, 4).reshape(own_p, QH, width)
    pulled_last = own_pulled[:, 0, :, heads].transpose(1, 0, 2).reshape(own_p, 1, width)
    pulled_rows = jnp.concatenate([pulled_heads, pulled_last], axis=1)
    folded = bottom_fold()
    to_send, folded, own_rows = lax.optimization_barrier((to_send, folded, pulled_rows))
    from_group = relay(to_send, 5)
    from_group, pulled_rows, all_loss = lax.optimization_barrier(
        (from_group, own_rows, all_loss)
    )
    pulled_below = lax.ppermute(pulled_rows, "section", [(1, 0)])

    above_heads = from_group[:, : n_p * heads].reshape(n_tensor, n_p, heads, cols)
    above_heads = above_heads.transpose(1, 0, 2, 3).reshape(n_p, QH, cols)
    above_pool = from_group[0, n_p * heads : n_p * heads + n_p]
    above_rows = jnp.concatenate([above_heads, above_pool[:, None, :]], axis=1)
    spread = lax.dot_general(
        above_rows.reshape(n_p * (QH + 1), cols),
        jnp.where(is_top, wo_below, wo[:half_cols]),
        (((1,), (1,)), ((), ())),
        preferred_element_type=F32,
    ).astype(BF16)
    spread = spread.reshape(n_dp, -1, 128)
    used = spread.shape[1]
    spread = jnp.pad(spread, ((0, 0), (0, round_up(used, 16) - used), (0, 0)))
    spread = scatter(spread, 10)[:, :used].reshape(2, seqs * (QH + 1), half_cols)
    spread = jnp.concatenate([spread[0], spread[1]], axis=1)
    spread = spread.reshape(seqs, QH + 1, kv, group, HEAD_SIZE)

    own_above = own_rows_of(picks_above)
    grad_top = jnp.einsum(
        "pet,ped->ptd",
        jnp.where(is_top, own_picks, own_above),
        jnp.where(is_top, pulled_rows, pulled_below),
        preferred_element_type=F32,
    )
    grad_top = grad_top.astype(BF16).reshape(rows, width)
    up_heads = up.reshape(rank, kv, HEAD_SIZE)
    up_top = adapter_scale * jnp.einsum(
        "pkga,pkgc->akc", picked_low.astype(BF16), grad_heads, preferred_element_type=F32
    ).reshape(rank, kv_cols)
    back_top = jnp.einsum(
        "pkgc,akc->pkga", grad_heads, up_heads, preferred_element_type=F32
    ).astype(BF16)
    down_top = adapter_scale * jnp.einsum(
        "pkga,pkgd->ad", back_top, picked_all, preferred_element_type=F32
    )

    grad_values = jnp.einsum(
        "pkgue,pekgc->pukc", folded, spread, preferred_element_type=F32
    ).astype(BF16)
    grad_values = grad_values.reshape(toks, kv_cols)
    term = lax.dot_general(
        grad_values, wv_all, (((1,), (1,)), ((), ())), preferred_element_type=F32
    ).astype(BF16)
    back = lax.dot_general(
        grad_values, up, (((1,), (1,)), ((), ())), preferred_element_type=F32
    ).astype(BF16)
    parts = exchange(
        jnp.concatenate([term, jnp.pad(back, ((0, 0), (0, 128 - rank)))], axis=1).reshape(
            n_tensor, rows, width + 128
        ),
        ("tensor",),
        7,
        section=0,
    )
    parts = jnp.sum(parts.astype(F32), axis=0)
    grad_bottom = (parts[:, :width] + grad_top.astype(F32)).astype(BF16)
    back_own = parts[:, width : width + rank].astype(BF16)
    down_low = adapter_scale * lax.dot_general(
        back_own, x, (((0,), (0,)), ((), ())), preferred_element_type=F32
    )
    up_low = adapter_scale * lax.dot_general(
        low_all, grad_values, (((0,), (0,)), ((), ())), preferred_element_type=F32
    )

    grad_input = jnp.where(is_top, grad_top, grad_bottom)
    down_top = lax.dynamic_update_slice_in_dim(
        jnp.zeros((rank, width), F32), down_top, di * cols, 1
    )
    grad_down = jnp.where(is_top, down_top, down_low)
    grad_up = jnp.where(is_top, jnp.where(di == 0, up_top, 0.0), up_low)
    ups = lax.dynamic_update_slice_in_dim(
        jnp.zeros((n_tensor, rank, kv_cols), F32), grad_up[None], ti, 0
    )
    grad_down, ups = total([grad_down, ups], ("dp", "tensor"), 8, None, BF16)
    grad_down, ups = grad_down.T.astype(F32), ups.astype(F32)
    grad_up = lax.dynamic_slice_in_dim(ups, ti, 1, 0)
    own_loss = lax.dynamic_slice_in_dim(all_loss, di * own_q, own_q, 0)
    below_loss = lax.ppermute(own_loss, "section", [(1, 0)])
    query_loss = jnp.where(is_top, own_loss, below_loss)
    return (query_loss, grad_input[None], grad_down[None], grad_up)


def solution(mesh):
    return jax.shard_map(
        on_device,
        mesh=mesh,
        in_specs=(
            P("section", ("dp", "tensor"), None),
            P("section", "dp", "tensor"),
            P("section", None, None),
            P("section", None, "tensor"),
            P("section", "tensor", "dp"),
            P("section", "dp", "tensor"),
            P("section", "dp", "tensor"),
            P("dp", None),
            P("dp"),
            P("dp", None),
            P("dp"),
        ),
        out_specs=(
            P("dp"),
            P("section", ("dp", "tensor"), None),
            P("section", None, None),
            P("section", None, "tensor"),
        ),
        check_vma=False,
    )
```

```python
import functools
import math

import jax
import jax.numpy as jnp
from jax import lax
from jax.experimental import pallas as pl
from jax.experimental.pallas import tpu as pltpu
from jax.sharding import PartitionSpec as P

HEAD_SIZE = 128
KEY_VALUE_HEADS = 8
QH = 32

tau_value = 0.02
adapter_scale = 2.0
loss_scale = 65536.0
tiny_eps = 1e-06
very_low = -1e30
HIGH = lax.Precision.HIGHEST
F32 = jnp.float32
BF16 = jnp.bfloat16
MESH = pl.DeviceIdType.MESH


def round_up(value, unit):
    return (value + unit - 1) // unit * unit


def place(axes, sizes):
    me = 0
    for axis, size in zip(axes, sizes):
        me = me * size + lax.axis_index(axis)

    def coords(index):
        out = {}
        for axis, size in reversed(list(zip(axes, sizes))):
            out[axis] = lax.rem(index, size)
            index = lax.div(index, size)
        return out

    return me, coords


def each_peer(n):
    def run(body):
        if n <= 16:
            for k in range(1, n):
                body(k)
        else:
            pl.loop(1, n)(body)

    return run


def enter(me, coords, n):
    barrier = pltpu.get_barrier_semaphore()

    @each_peer(n)
    def _(k):
        pl.semaphore_signal(
            barrier, inc=1, device_id=coords(lax.rem(me + k, n)), device_id_type=MESH
        )

    pl.semaphore_wait(barrier, n - 1)


def push_all(me, coords, n, source, target, send_sem, recv_sem):
    def copy(k, to_index, slot):
        return pltpu.make_async_remote_copy(
            src_ref=source(to_index),
            dst_ref=target.at[slot],
            send_sem=send_sem.at[k],
            recv_sem=recv_sem.at[k],
            device_id=coords(to_index),
            device_id_type=MESH,
        )

    @each_peer(n)
    def _(k):
        copy(k, lax.rem(me + k, n), me).start()

    @each_peer(n)
    def _(k):
        copy(k, lax.rem(me + k, n), lax.rem(me + n - k, n)).wait()


def params(cid, *arrays):
    need = sum(math.prod(a.shape) * a.dtype.itemsize for a in arrays)
    return dict(
        compiler_params=pltpu.CompilerParams(
            collective_id=cid, has_side_effects=True, vmem_limit_bytes=need * 5 // 4 + 2 * 1024 * 1024
        ),
        cost_estimate=pl.CostEstimate(
            flops=0, bytes_accessed=32 * 1024 * 1024, transcendentals=0
        ),
    )


def vmem(count):
    return [pl.BlockSpec(memory_space=pltpu.VMEM)] * count


def in_section(section, out_ref, run):
    if section is None:
        run()
        return
    here = lax.axis_index("section") == section
    pl.when(here)(run)

    @pl.when(jnp.logical_not(here))
    def _():
        out_ref[...] = jnp.zeros_like(out_ref)


def exchange_kernel(axes, sizes, same, section, x_ref, out_ref, send_sem, recv_sem):
    n = math.prod(sizes)

    def run():
        me, coords = place(axes, sizes)
        enter(me, coords, n)
        source = (lambda to: x_ref) if same else (lambda to: x_ref.at[to])
        out_ref[me] = x_ref[...] if same else x_ref[me]
        push_all(me, coords, n, source, out_ref, send_sem, recv_sem)

    in_section(section, out_ref, run)


def exchange(x, axes, cid, same=False, section=None):
    sizes = tuple(lax.axis_size(axis) for axis in axes)
    n = math.prod(sizes)
    shape = (n,) + x.shape if same else x.shape
    return pl.pallas_call(
        functools.partial(exchange_kernel, axes, sizes, same, section),
        out_shape=jax.ShapeDtypeStruct(shape, x.dtype),
        in_specs=vmem(1),
        out_specs=vmem(1)[0],
        scratch_shapes=[pltpu.SemaphoreType.DMA((n,)), pltpu.SemaphoreType.DMA((n,))],
        **params(cid, x, jax.ShapeDtypeStruct(shape, x.dtype)),
    )(x)


def total_kernel(axes, sizes, section, x_ref, out_ref, held, send_a, recv_a, send_b, recv_b):
    n = math.prod(sizes)

    def run():
        me, coords = place(axes, sizes)
        enter(me, coords, n)
        held[me] = x_ref[me]
        push_all(me, coords, n, lambda to: x_ref.at[to], held, send_a, recv_a)
        out_ref[me] = jnp.sum(held[...].astype(F32), axis=0).astype(out_ref.dtype)
        push_all(me, coords, n, lambda to: out_ref.at[me], out_ref, send_b, recv_b)

    in_section(section, out_ref, run)


def total(arrays, axes, cid, section=None, dtype=F32):
    sizes = tuple(lax.axis_size(axis) for axis in axes)
    n = math.prod(sizes)
    flat = [a.reshape(-1).astype(dtype) for a in arrays]
    count = sum(a.size for a in flat)
    share = round_up(-(-count // n), 1024 if dtype == F32 else 2048)
    packed = jnp.concatenate(flat + [jnp.zeros((share * n - count,), dtype)])
    packed = packed.reshape(n, share // 128, 128)
    out = pl.pallas_call(
        functools.partial(total_kernel, axes, sizes, section),
        out_shape=jax.ShapeDtypeStruct(packed.shape, dtype),
        in_specs=vmem(1),
        out_specs=vmem(1)[0],
        scratch_shapes=[pltpu.VMEM(packed.shape, dtype)]
        + [pltpu.SemaphoreType.DMA((n,)) for _ in range(4)],
        **params(cid, packed, packed, packed),
    )(packed).reshape(-1)
    results, at = [], 0
    for a in arrays:
        results.append(out[at : at + a.size].reshape(a.shape))
        at += a.size
    return results


def opening_kernel(
    sizes,
    x_ref,
    wv_ref,
    wo_ref,
    picks_ref,
    got_ref,
    all_ref,
    below_ref,
    above_ref,
    send_sem,
    recv_sem,
    send_a,
    recv_a,
    send_b,
    recv_b,
    cross,
):
    n, n_dp = math.prod(sizes), sizes[0]
    half = n_dp // 2
    section = lax.axis_index("section")
    me, coords = place(("dp", "tensor"), sizes)
    barrier = pltpu.get_barrier_semaphore()
    pl.semaphore_signal(
        barrier, inc=1, device_id={"section": 1 - section}, device_id_type=MESH
    )

    @each_peer(n)
    def _(k):
        pl.semaphore_signal(
            barrier, inc=1, device_id=coords(lax.rem(me + k, n)), device_id_type=MESH
        )

    pl.semaphore_wait(barrier, n)

    def crossing(source, target, first, to):
        return pltpu.make_async_remote_copy(
            src_ref=source,
            dst_ref=target,
            send_sem=cross.at[first],
            recv_sem=cross.at[first + 1],
            device_id={"section": to},
            device_id_type=MESH,
        )

    rows = below_ref.shape[0]
    picks_down = crossing(picks_ref, above_ref, 0, 0)
    weight_up = crossing(wo_ref.at[pl.ds(rows, rows)], below_ref, 2, 1)

    @pl.when(section == 1)
    def _():
        picks_down.start()
        got_ref[me] = x_ref[me]
        push_all(me, coords, n, lambda to: x_ref.at[to], got_ref, send_sem, recv_sem)
        picks_down.wait_send()
        weight_up.wait_recv()

    @pl.when(section == 0)
    def _():
        weight_up.start()
        di = lax.axis_index("dp")
        partner = di + 1 - 2 * lax.rem(di, 2)
        line = lax.div(di, 2)
        own = pltpu.make_async_copy(wv_ref, all_ref.at[di], cross.at[4])
        own.start()

        def along(j, step, slot):
            index = j if step > 0 else half + j
            return pltpu.make_async_remote_copy(
                src_ref=wv_ref if j == 0 else all_ref.at[slot],
                dst_ref=all_ref.at[slot],
                send_sem=send_a.at[index],
                recv_sem=recv_a.at[index],
                device_id={"dp": di + 2 * step},
                device_id_type=MESH,
            )

        def across(j, step, slot):
            index = j if step > 0 else half + j
            return pltpu.make_async_remote_copy(
                src_ref=wv_ref if j == 0 else all_ref.at[slot],
                dst_ref=all_ref.at[slot],
                send_sem=send_b.at[index],
                recv_sem=recv_b.at[index],
                device_id={"dp": partner},
                device_id_type=MESH,
            )

        def has_next(step):
            return line < half - 1 if step > 0 else line > 0

        def has_slot(j, step):
            return line >= j if step > 0 else line + j < half

        across(0, 1, di).start()
        for step in (1, -1):
            pl.when(has_next(step))(lambda step=step: along(0, step, di).start())
        got_ref[...] = jnp.zeros_like(got_ref)
        for j in range(1, half):
            for step in (1, -1):

                @pl.when(has_slot(j, step))
                def _(j=j, step=step):
                    slot = di - 2 * j * step
                    along(j - 1, step, slot).wait_recv()
                    across(j, step, slot).start()
                    pl.when(has_next(step))(lambda: along(j, step, slot).start())

        own.wait()
        across(0, 1, partner).wait()
        for step in (1, -1):
            pl.when(has_next(step))(lambda step=step: along(0, step, di).wait_send())
        for j in range(1, half):
            for step in (1, -1):

                @pl.when(has_slot(j, step))
                def _(j=j, step=step):
                    slot = di - 2 * j * step
                    across(j, step, partner - 2 * j * step).wait_recv()
                    across(j, step, slot).wait_send()
                    pl.when(has_next(step))(lambda: along(j, step, slot).wait_send())

        weight_up.wait_send()
        picks_down.wait_recv()


def opening(x, wv, wo, picks, cid):
    sizes = (lax.axis_size("dp"), lax.axis_size("tensor"))
    n, n_dp = math.prod(sizes), sizes[0]
    shape = jax.ShapeDtypeStruct
    hbm = pl.BlockSpec(memory_space=pl.ANY)
    return pl.pallas_call(
        functools.partial(opening_kernel, sizes),
        out_shape=(
            shape(x.shape, x.dtype),
            shape((n_dp,) + wv.shape, wv.dtype),
            shape((wo.shape[0] // 2, wo.shape[1]), wo.dtype),
            shape(picks.shape, picks.dtype),
        ),
        in_specs=vmem(1) + [hbm, hbm] + vmem(1),
        out_specs=tuple(vmem(1) + [hbm, hbm] + vmem(1)),
        scratch_shapes=[pltpu.SemaphoreType.DMA((n,)) for _ in range(2)]
        + [pltpu.SemaphoreType.DMA((n_dp,)) for _ in range(4)]
        + [pltpu.SemaphoreType.DMA((5,))],
        **params(cid, x, x, picks, picks),
    )(x, wv, wo, picks)


def relay_kernel(n, x_ref, out_ref, send_sem, recv_sem, down_sem):
    ti = lax.axis_index("tensor")
    section = lax.axis_index("section")
    barrier = pltpu.get_barrier_semaphore()
    pl.semaphore_signal(
        barrier, inc=1, device_id={"section": 1 - section}, device_id_type=MESH
    )

    @each_peer(n)
    def _(k):
        pl.semaphore_signal(
            barrier, inc=1, device_id={"tensor": lax.rem(ti + k, n)}, device_id_type=MESH
        )

    pl.semaphore_wait(barrier, n)
    down = pltpu.make_async_remote_copy(
        src_ref=x_ref,
        dst_ref=out_ref.at[ti],
        send_sem=down_sem.at[0],
        recv_sem=down_sem.at[1],
        device_id={"section": 0},
        device_id_type=MESH,
    )
    coords = lambda index: {"tensor": index}

    @pl.when(section == 1)
    def _():
        down.start()
        out_ref[ti] = x_ref[...]
        push_all(ti, coords, n, lambda to: x_ref, out_ref, send_sem, recv_sem)
        down.wait_send()

    @pl.when(section == 0)
    def _():
        down.wait_recv()
        push_all(ti, coords, n, lambda to: out_ref.at[ti], out_ref, send_sem, recv_sem)


def relay(x, cid):
    n = lax.axis_size("tensor")
    return pl.pallas_call(
        functools.partial(relay_kernel, n),
        out_shape=jax.ShapeDtypeStruct((n,) + x.shape, x.dtype),
        in_specs=vmem(1),
        out_specs=vmem(1)[0],
        scratch_shapes=[pltpu.SemaphoreType.DMA((max(n, 2),)) for _ in range(3)],
        **params(cid, x, jax.ShapeDtypeStruct((n,) + x.shape, x.dtype)),
    )(x)


def scatter_kernel(n, x_ref, out_ref, held, send_a, recv_a, down_sem):
    me, coords = place(("dp",), (n,))
    section = lax.axis_index("section")
    barrier = pltpu.get_barrier_semaphore()
    pl.semaphore_signal(
        barrier, inc=1, device_id={"section": 1 - section}, device_id_type=MESH
    )

    @each_peer(n)
    def _(k):
        pl.semaphore_signal(
            barrier, inc=1, device_id=coords(lax.rem(me + k, n)), device_id_type=MESH
        )

    pl.semaphore_wait(barrier, n)
    held[me] = x_ref[me]
    push_all(me, coords, n, lambda to: x_ref.at[to], held, send_a, recv_a)
    out_ref[section] = jnp.sum(held[...].astype(F32), axis=0).astype(out_ref.dtype)
    down = pltpu.make_async_remote_copy(
        src_ref=out_ref.at[1],
        dst_ref=out_ref.at[1],
        send_sem=down_sem.at[0],
        recv_sem=down_sem.at[1],
        device_id={"section": 0},
        device_id_type=MESH,
    )

    @pl.when(section == 1)
    def _():
        out_ref[0] = jnp.zeros_like(out_ref[0])
        down.start()
        down.wait_send()

    @pl.when(section == 0)
    def _():
        down.wait_recv()


def scatter(x, cid):
    n = lax.axis_size("dp")
    return pl.pallas_call(
        functools.partial(scatter_kernel, n),
        out_shape=jax.ShapeDtypeStruct((2,) + x.shape[1:], x.dtype),
        in_specs=vmem(1),
        out_specs=vmem(1)[0],
        scratch_shapes=[pltpu.VMEM(x.shape, x.dtype)]
        + [pltpu.SemaphoreType.DMA((n,)) for _ in range(2)]
        + [pltpu.SemaphoreType.DMA((2,))],
        **params(cid, x, x, x),
    )(x)


def on_device(
    section_layer_input,
    value_projection_weight,
    adapter_down_weight,
    adapter_up_weight,
    output_weight,
    rotated_query_cache,
    rotated_key_cache,
    query_embedding,
    positives,
    hard_negative_passages,
    lengths,
):
    n_dp, n_tensor = lax.axis_size("dp"), lax.axis_size("tensor")
    is_top = lax.axis_index("section") == 1
    ti, di = lax.axis_index("tensor"), lax.axis_index("dp")
    x = section_layer_input[0]
    wv, down, up, wo = (
        value_projection_weight[0],
        adapter_down_weight[0],
        adapter_up_weight[0],
        output_weight[0],
    )
    rows, width = x.shape
    seqs = lengths.shape[0]
    toks = rows * n_tensor
    seq_len = toks // seqs
    cols = wv.shape[0]
    kv_cols = wv.shape[1]
    kv = kv_cols // HEAD_SIZE
    group = QH // KEY_VALUE_HEADS
    heads = kv * group
    rank = down.shape[1]
    own_q = query_embedding.shape[0]
    n_neg = hard_negative_passages.shape[1]
    n_q, n_p = n_dp * own_q, n_dp * seqs
    own_p = max(1, rows // seq_len)
    share = n_tensor * own_p // seqs
    own_first = ti * rows // seq_len

    down_cols = lax.dynamic_slice_in_dim(down, di * cols, cols, 0)
    wvf = (
        wv.astype(F32) + adapter_scale * jnp.dot(down_cols, up, preferred_element_type=F32)
    ).astype(BF16)
    wv_heads = wvf.reshape(cols, kv, HEAD_SIZE)
    half_cols = wo.shape[0] // 2

    positions = jnp.arange(seq_len, dtype=jnp.int32)
    is_valid = positions[None, :] < lengths[:, None]
    last_pick = (positions[None, :] == lengths[:, None] - 1).astype(BF16)
    query_grid = rotated_query_cache[0].reshape(seqs, seq_len, kv, group, HEAD_SIZE)
    key_grid = rotated_key_cache[0].reshape(seqs, seq_len, kv, HEAD_SIZE)
    last_query = jnp.einsum(
        "pt,pthd->phd",
        last_pick,
        rotated_query_cache[0].reshape(seqs, seq_len, heads, HEAD_SIZE),
        preferred_element_type=F32,
    ).astype(BF16)
    scores = jnp.einsum(
        "pkgd,ptkd->pkgt",
        last_query.reshape(seqs, kv, group, HEAD_SIZE),
        key_grid,
        preferred_element_type=F32,
    ) / math.sqrt(HEAD_SIZE)
    scores = jnp.where(is_valid[:, None, None, :], scores, very_low)
    probs_top = jax.nn.softmax(scores, axis=-1).astype(BF16)
    low = jnp.dot(x, down, preferred_element_type=F32).astype(BF16)
    probs_rows = probs_top.reshape(seqs * heads, seq_len)
    pad_rows = round_up(seqs * heads, 16)
    probs_rows = jnp.pad(probs_rows, ((0, pad_rows - seqs * heads), (0, 0)))
    low_rows = jnp.pad(low, ((0, 0), (0, seq_len - rank)))
    probs_all = exchange(
        jnp.concatenate([probs_rows, low_rows], axis=0), ("tensor",), 0, same=True
    )
    low_all = probs_all[:, pad_rows : pad_rows + rows, :rank].reshape(toks, rank)
    probs_all = probs_all[:, : seqs * heads]
    probs_all = probs_all.reshape(n_tensor, seqs, heads, seq_len).transpose(1, 0, 2, 3)
    picks = jnp.concatenate(
        [probs_all.reshape(seqs, QH, seq_len), last_pick[:, None, :]], axis=1
    )

    def fold():
        scores_low = jnp.einsum(
            "ptkgd,pukd->pkgtu", query_grid, key_grid, preferred_element_type=F32
        ) / math.sqrt(HEAD_SIZE)
        allowed = (positions[None, :, None] >= positions[None, None, :]) & is_valid[:, None, :]
        scores_low = jnp.where(allowed[:, None, None, :, :], scores_low, very_low)
        probs_low = jax.nn.softmax(scores_low, axis=-1).astype(BF16)
        return jnp.einsum(
            "pkgtu,pet->pkgue", probs_low, picks_above, preferred_element_type=F32
        ).astype(BF16)

    def bottom_fold():
        shape = (seqs, kv, group, seq_len, QH + 1)
        return lax.cond(is_top, lambda: jnp.zeros(shape, BF16), fold)

    def own_rows_of(full):
        part = lax.dynamic_slice_in_dim(full, own_first, own_p, 0)
        if share > 1:
            part = lax.dynamic_slice_in_dim(part, (ti % share) * rows, rows, 2)
        return part

    own_picks = own_rows_of(picks)
    picked = jnp.einsum(
        "pet,ptd->ped",
        own_picks,
        x.reshape(own_p, rows // own_p, width),
        preferred_element_type=F32,
    ).astype(BF16)
    by_block = picked.reshape(own_p, QH + 1, n_dp, cols).transpose(2, 0, 1, 3)
    head_part = by_block[:, :, :QH].reshape(n_dp, own_p, n_tensor, heads, cols)
    head_part = head_part.transpose(0, 2, 1, 3, 4).reshape(n_dp, n_tensor, own_p * heads, cols)
    last_part = by_block[:, :, QH]
    query_part = query_embedding.reshape(own_q, n_dp, cols).transpose(1, 0, 2)
    numbers = jnp.concatenate([positives[:, None], hard_negative_passages], axis=1)
    numbers = jnp.pad(numbers.astype(BF16), ((0, 0), (0, cols - 1 - n_neg)))
    numbers = jnp.broadcast_to(numbers[None], (n_dp, own_q, cols))
    tail = jnp.concatenate([last_part, query_part, numbers], axis=1)
    tail = jnp.broadcast_to(tail[:, None], (n_dp, n_tensor) + tail.shape[1:])
    message = jnp.concatenate([head_part, tail], axis=2)
    used = message.shape[2]
    message = jnp.pad(message, ((0, 0), (0, 0), (0, round_up(used, 16) - used), (0, 0)))
    pad_picks = jnp.pad(picks, ((0, 0), (0, round_up(QH + 1, 16) - QH - 1), (0, 0)))
    got, wv_all, wo_below, picks_above = opening(
        message.reshape((n_dp * n_tensor,) + message.shape[2:]), wvf, wo, pad_picks, 1
    )
    wv_all = wv_all.reshape(width, kv_cols)
    picks_above = picks_above[:, : QH + 1]
    got = got.reshape((n_dp, n_tensor) + got.shape[1:])
    first = own_p * heads

    def by_passage(part, count):
        part = part.reshape(n_dp, n_tensor // share, share, own_p, count, cols)
        if share > 1:
            part = jnp.sum(part.astype(F32), axis=2).astype(BF16)
        return part.reshape(n_p, count, cols)

    picked_all = by_passage(got[:, :, :first], heads).reshape(n_p, kv, group, cols)
    last_in = by_passage(got[:, :, first : first + own_p], 1)[:, 0].astype(F32)
    queries = got[:, 0, first + own_p : first + own_p + own_q].reshape(n_q, cols)
    numbers = got[:, 0, first + own_p + own_q : first + own_p + 2 * own_q].reshape(n_q, cols)
    all_pos = numbers[:, 0].astype(jnp.int32)
    all_neg = numbers[:, 1 : 1 + n_neg].astype(jnp.int32)

    attended = jnp.einsum("pkgd,dkc->pkgc", picked_all, wv_heads, preferred_element_type=F32)
    picked_low = jnp.einsum("pkgd,da->pkga", picked_all, down_cols, preferred_element_type=F32)
    attended, picked_low = total([attended, picked_low], ("dp",), 2, 1, BF16)
    attended = attended.reshape(n_p, heads * HEAD_SIZE).astype(BF16)
    mixed = jnp.dot(attended, wo, preferred_element_type=F32)
    mixed_rows = jnp.pad(mixed, ((0, round_up(n_p, 8) - n_p), (0, 0)))
    mixed = jnp.sum(exchange(mixed_rows, ("tensor",), 3, same=True, section=1), axis=0)[:n_p]
    pooled = last_in + mixed

    query_f = queries.astype(F32)
    pooled_hi = pooled.astype(BF16)
    pooled_lo = (pooled - pooled_hi.astype(F32)).astype(BF16)
    products = lax.dot_general(
        jnp.concatenate([queries, pooled_hi, pooled_lo], axis=0),
        wo,
        (((1,), (1,)), ((), ())),
        preferred_element_type=F32,
    )
    prod_q = products[:n_q]
    prod_p = products[n_q : n_q + n_p] + products[n_q + n_p :]
    dots = jnp.dot(query_f, pooled.T, precision=HIGH)
    prod_q, prod_p, dots, query_sq, pooled_sq = total(
        [prod_q, prod_p, dots, jnp.sum(query_f * query_f, -1), jnp.sum(pooled * pooled, -1)],
        ("dp",),
        4,
        1,
    )
    query_norm = jnp.sqrt(query_sq + tiny_eps)[:, None]
    pooled_norm = jnp.sqrt(pooled_sq + tiny_eps)[None, :]
    cosines = dots / query_norm / pooled_norm
    logits = cosines / tau_value
    passage_ids = jnp.arange(n_p, dtype=jnp.int32)
    pos_hot = (all_pos[:, None] == passage_ids[None, :]).astype(F32)
    is_positive = jnp.any(all_pos[:, None] == passage_ids[None, :], axis=0)
    is_negative = jnp.any(all_neg[:, :, None] == passage_ids[None, None, :], axis=1)
    candidate = is_positive[None, :] | is_negative
    row_max = jnp.max(jnp.where(candidate, logits, very_low), axis=-1)
    row_total = jnp.sum(jnp.where(candidate, jnp.exp(logits - row_max[:, None]), 0.0), axis=-1)
    row_lse = row_max + jnp.log(row_total)
    all_loss = row_lse - jnp.sum(pos_hot * logits, axis=-1)
    weights = jnp.where(candidate, jnp.exp(logits - row_lse[:, None]), 0.0) - pos_hot
    weights = weights * (loss_scale / (n_q * tau_value))
    along = jnp.sum(weights * cosines, axis=0)
    norm = pooled_norm[0][:, None]
    coef_q = (weights / query_norm).T / norm
    coef_p = along[:, None] / (norm * norm)
    grad_pool = (jnp.dot(coef_q, query_f, precision=HIGH) - coef_p * pooled).astype(BF16)
    grad_att = (jnp.dot(coef_q, prod_q, precision=HIGH) - coef_p * prod_p).astype(BF16)

    grad_heads = grad_att.reshape(n_p, kv, group, HEAD_SIZE)
    pulled = jnp.einsum("pkgc,dkc->pkgd", grad_heads, wv_heads, preferred_element_type=F32)
    pulled = pulled.astype(BF16).reshape(n_p, heads, cols)
    to_send = jnp.concatenate([pulled.reshape(n_p * heads, cols), grad_pool], axis=0)
    to_send = jnp.pad(to_send, ((0, round_up(to_send.shape[0], 16) - to_send.shape[0]), (0, 0)))
    pulled = jnp.concatenate([pulled, grad_pool[:, None, :]], axis=1)
    pulled = pulled.reshape(n_dp, n_tensor // share, own_p * (heads + 1), cols)
    used = own_p * (heads + 1)
    pulled = jnp.pad(pulled, ((0, 0), (0, 0), (0, round_up(used, 16) - used), (0, 0)))
    pulled = jnp.repeat(pulled, share, axis=1)
    own_pulled = exchange(
        pulled.reshape((n_dp * n_tensor,) + pulled.shape[2:]), ("dp", "tensor"), 6, section=1
    )[:, :used]
    own_pulled = own_pulled.reshape(n_dp, n_tensor, own_p, heads + 1, cols)
    pulled_heads = own_pulled[:, :, :, :heads].transpose(2, 1, 3, 0, 4).reshape(own_p, QH, width)
    pulled_last = own_pulled[:, 0, :, heads].transpose(1, 0, 2).reshape(own_p, 1, width)
    pulled_rows = jnp.concatenate([pulled_heads, pulled_last], axis=1)
    folded = bottom_fold()
    to_send, folded, own_rows = lax.optimization_barrier((to_send, folded, pulled_rows))
    from_group = relay(to_send, 5)
    from_group, pulled_rows, all_loss = lax.optimization_barrier(
        (from_group, own_rows, all_loss)
    )
    pulled_below = lax.ppermute(pulled_rows, "section", [(1, 0)])

    above_heads = from_group[:, : n_p * heads].reshape(n_tensor, n_p, heads, cols)
    above_heads = above_heads.transpose(1, 0, 2, 3).reshape(n_p, QH, cols)
    above_pool = from_group[0, n_p * heads : n_p * heads + n_p]
    above_rows = jnp.concatenate([above_heads, above_pool[:, None, :]], axis=1)
    spread = lax.dot_general(
        above_rows.reshape(n_p * (QH + 1), cols),
        jnp.where(is_top, wo_below, wo[:half_cols]),
        (((1,), (1,)), ((), ())),
        preferred_element_type=F32,
    ).astype(BF16)
    spread = spread.reshape(n_dp, -1, 128)
    used = spread.shape[1]
    spread = jnp.pad(spread, ((0, 0), (0, round_up(used, 16) - used), (0, 0)))
    spread = scatter(spread, 10)[:, :used].reshape(2, seqs * (QH + 1), half_cols)
    spread = jnp.concatenate([spread[0], spread[1]], axis=1)
    spread = spread.reshape(seqs, QH + 1, kv, group, HEAD_SIZE)

    own_above = own_rows_of(picks_above)
    grad_top = jnp.einsum(
        "pet,ped->ptd",
        jnp.where(is_top, own_picks, own_above),
        jnp.where(is_top, pulled_rows, pulled_below),
        preferred_element_type=F32,
    )
    grad_top = grad_top.astype(BF16).reshape(rows, width)
    up_heads = up.reshape(rank, kv, HEAD_SIZE)
    up_top = adapter_scale * jnp.einsum(
        "pkga,pkgc->akc", picked_low.astype(BF16), grad_heads, preferred_element_type=F32
    ).reshape(rank, kv_cols)
    back_top = jnp.einsum(
        "pkgc,akc->pkga", grad_heads, up_heads, preferred_element_type=F32
    ).astype(BF16)
    down_top = adapter_scale * jnp.einsum(
        "pkga,pkgd->ad", back_top, picked_all, preferred_element_type=F32
    )

    grad_values = jnp.einsum(
        "pkgue,pekgc->pukc", folded, spread, preferred_element_type=F32
    ).astype(BF16)
    grad_values = grad_values.reshape(toks, kv_cols)
    term = lax.dot_general(
        grad_values, wv_all, (((1,), (1,)), ((), ())), preferred_element_type=F32
    ).astype(BF16)
    back = lax.dot_general(
        grad_values, up, (((1,), (1,)), ((), ())), preferred_element_type=F32
    ).astype(BF16)
    parts = exchange(
        jnp.concatenate([term, jnp.pad(back, ((0, 0), (0, 128 - rank)))], axis=1).reshape(
            n_tensor, rows, width + 128
        ),
        ("tensor",),
        7,
        section=0,
    )
    parts = jnp.sum(parts.astype(F32), axis=0)
    grad_bottom = (parts[:, :width] + grad_top.astype(F32)).astype(BF16)
    back_own = parts[:, width : width + rank].astype(BF16)
    down_low = adapter_scale * lax.dot_general(
        back_own, x, (((0,), (0,)), ((), ())), preferred_element_type=F32
    )
    up_low = adapter_scale * lax.dot_general(
        low_all, grad_values, (((0,), (0,)), ((), ())), preferred_element_type=F32
    )

    grad_input = jnp.where(is_top, grad_top, grad_bottom)
    down_top = lax.dynamic_update_slice_in_dim(
        jnp.zeros((rank, width), F32), down_top, di * cols, 1
    )
    grad_down = jnp.where(is_top, down_top, down_low)
    grad_up = jnp.where(is_top, jnp.where(di == 0, up_top, 0.0), up_low)
    ups = lax.dynamic_update_slice_in_dim(
        jnp.zeros((n_tensor, rank, kv_cols), F32), grad_up[None], ti, 0
    )
    grad_down, ups = total([grad_down, ups], ("dp", "tensor"), 8, None, BF16)
    grad_down, ups = grad_down.T.astype(F32), ups.astype(F32)
    grad_up = lax.dynamic_slice_in_dim(ups, ti, 1, 0)
    own_loss = lax.dynamic_slice_in_dim(all_loss, di * own_q, own_q, 0)
    below_loss = lax.ppermute(own_loss, "section", [(1, 0)])
    query_loss = jnp.where(is_top, own_loss, below_loss)
    return (query_loss, grad_input[None], grad_down[None], grad_up)


def solution(mesh):
    return jax.shard_map(
        on_device,
        mesh=mesh,
        in_specs=(
            P("section", ("dp", "tensor"), None),
            P("section", "dp", "tensor"),
            P("section", None, None),
            P("section", None, "tensor"),
            P("section", "tensor", "dp"),
            P("section", "dp", "tensor"),
            P("section", "dp", "tensor"),
            P("dp", None),
            P("dp"),
            P("dp", None),
            P("dp"),
        ),
        out_specs=(
            P("dp"),
            P("section", ("dp", "tensor"), None),
            P("section", None, None),
            P("section", None, "tensor"),
        ),
        check_vma=False,
    )
```

```python
import functools
import math

import jax
import jax.numpy as jnp
from jax import lax
from jax.experimental import pallas as pl
from jax.experimental.pallas import tpu as pltpu
from jax.sharding import PartitionSpec as P

HEAD_SIZE = 128
KEY_VALUE_HEADS = 8
QH = 32

tau_value = 0.02
adapter_scale = 2.0
loss_scale = 65536.0
tiny_eps = 1e-06
very_low = -1e30
HIGH = lax.Precision.HIGHEST
F32 = jnp.float32
BF16 = jnp.bfloat16
MESH = pl.DeviceIdType.MESH


def round_up(value, unit):
    return (value + unit - 1) // unit * unit


def place(axes, sizes):
    me = 0
    for axis, size in zip(axes, sizes):
        me = me * size + lax.axis_index(axis)

    def coords(index):
        out = {}
        for axis, size in reversed(list(zip(axes, sizes))):
            out[axis] = lax.rem(index, size)
            index = lax.div(index, size)
        return out

    return me, coords


def each_peer(n):
    def run(body):
        if n <= 16:
            for k in range(1, n):
                body(k)
        else:
            pl.loop(1, n)(body)

    return run


def enter(me, coords, n):
    barrier = pltpu.get_barrier_semaphore()

    @each_peer(n)
    def _(k):
        pl.semaphore_signal(
            barrier, inc=1, device_id=coords(lax.rem(me + k, n)), device_id_type=MESH
        )

    pl.semaphore_wait(barrier, n - 1)


def push_all(me, coords, n, source, target, send_sem, recv_sem):
    def copy(k, to_index, slot):
        return pltpu.make_async_remote_copy(
            src_ref=source(to_index),
            dst_ref=target.at[slot],
            send_sem=send_sem.at[k],
            recv_sem=recv_sem.at[k],
            device_id=coords(to_index),
            device_id_type=MESH,
        )

    @each_peer(n)
    def _(k):
        copy(k, lax.rem(me + k, n), me).start()

    @each_peer(n)
    def _(k):
        copy(k, lax.rem(me + k, n), lax.rem(me + n - k, n)).wait()


def params(cid, *arrays):
    need = sum(math.prod(a.shape) * a.dtype.itemsize for a in arrays)
    return dict(
        compiler_params=pltpu.CompilerParams(
            collective_id=cid, has_side_effects=True, vmem_limit_bytes=need * 5 // 4 + 2 * 1024 * 1024
        ),
        cost_estimate=pl.CostEstimate(
            flops=0, bytes_accessed=32 * 1024 * 1024, transcendentals=0
        ),
    )


def vmem(count):
    return [pl.BlockSpec(memory_space=pltpu.VMEM)] * count


def in_section(section, out_ref, run):
    if section is None:
        run()
        return
    here = lax.axis_index("section") == section
    pl.when(here)(run)

    @pl.when(jnp.logical_not(here))
    def _():
        out_ref[...] = jnp.zeros_like(out_ref)


def exchange_kernel(axes, sizes, same, section, x_ref, out_ref, send_sem, recv_sem):
    n = math.prod(sizes)

    def run():
        me, coords = place(axes, sizes)
        enter(me, coords, n)
        source = (lambda to: x_ref) if same else (lambda to: x_ref.at[to])
        out_ref[me] = x_ref[...] if same else x_ref[me]
        push_all(me, coords, n, source, out_ref, send_sem, recv_sem)

    in_section(section, out_ref, run)


def exchange(x, axes, cid, same=False, section=None):
    sizes = tuple(lax.axis_size(axis) for axis in axes)
    n = math.prod(sizes)
    shape = (n,) + x.shape if same else x.shape
    return pl.pallas_call(
        functools.partial(exchange_kernel, axes, sizes, same, section),
        out_shape=jax.ShapeDtypeStruct(shape, x.dtype),
        in_specs=vmem(1),
        out_specs=vmem(1)[0],
        scratch_shapes=[pltpu.SemaphoreType.DMA((n,)), pltpu.SemaphoreType.DMA((n,))],
        **params(cid, x, jax.ShapeDtypeStruct(shape, x.dtype)),
    )(x)


def total_kernel(axes, sizes, section, x_ref, out_ref, held, send_a, recv_a, send_b, recv_b):
    n = math.prod(sizes)

    def run():
        me, coords = place(axes, sizes)
        enter(me, coords, n)
        held[me] = x_ref[me]
        push_all(me, coords, n, lambda to: x_ref.at[to], held, send_a, recv_a)
        out_ref[me] = jnp.sum(held[...].astype(F32), axis=0).astype(out_ref.dtype)
        push_all(me, coords, n, lambda to: out_ref.at[me], out_ref, send_b, recv_b)

    in_section(section, out_ref, run)


def total(arrays, axes, cid, section=None, dtype=F32):
    sizes = tuple(lax.axis_size(axis) for axis in axes)
    n = math.prod(sizes)
    flat = [a.reshape(-1).astype(dtype) for a in arrays]
    count = sum(a.size for a in flat)
    share = round_up(-(-count // n), 1024 if dtype == F32 else 2048)
    packed = jnp.concatenate(flat + [jnp.zeros((share * n - count,), dtype)])
    packed = packed.reshape(n, share // 128, 128)
    out = pl.pallas_call(
        functools.partial(total_kernel, axes, sizes, section),
        out_shape=jax.ShapeDtypeStruct(packed.shape, dtype),
        in_specs=vmem(1),
        out_specs=vmem(1)[0],
        scratch_shapes=[pltpu.VMEM(packed.shape, dtype)]
        + [pltpu.SemaphoreType.DMA((n,)) for _ in range(4)],
        **params(cid, packed, packed, packed),
    )(packed).reshape(-1)
    results, at = [], 0
    for a in arrays:
        results.append(out[at : at + a.size].reshape(a.shape))
        at += a.size
    return results


def opening_kernel(
    sizes,
    x_ref,
    wv_ref,
    wo_ref,
    picks_ref,
    got_ref,
    all_ref,
    below_ref,
    above_ref,
    send_sem,
    recv_sem,
    send_a,
    recv_a,
    send_b,
    recv_b,
    cross,
):
    n, n_dp = math.prod(sizes), sizes[0]
    half = n_dp // 2
    section = lax.axis_index("section")
    me, coords = place(("dp", "tensor"), sizes)
    barrier = pltpu.get_barrier_semaphore()
    pl.semaphore_signal(
        barrier, inc=1, device_id={"section": 1 - section}, device_id_type=MESH
    )

    @each_peer(n)
    def _(k):
        pl.semaphore_signal(
            barrier, inc=1, device_id=coords(lax.rem(me + k, n)), device_id_type=MESH
        )

    pl.semaphore_wait(barrier, n)

    def crossing(source, target, first, to):
        return pltpu.make_async_remote_copy(
            src_ref=source,
            dst_ref=target,
            send_sem=cross.at[first],
            recv_sem=cross.at[first + 1],
            device_id={"section": to},
            device_id_type=MESH,
        )

    rows = below_ref.shape[0]
    picks_down = crossing(picks_ref, above_ref, 0, 0)
    weight_up = crossing(wo_ref.at[pl.ds(rows, rows)], below_ref, 2, 1)

    @pl.when(section == 1)
    def _():
        picks_down.start()
        got_ref[me] = x_ref[me]
        push_all(me, coords, n, lambda to: x_ref.at[to], got_ref, send_sem, recv_sem)
        picks_down.wait_send()
        weight_up.wait_recv()

    @pl.when(section == 0)
    def _():
        weight_up.start()
        di = lax.axis_index("dp")
        partner = di + 1 - 2 * lax.rem(di, 2)
        line = lax.div(di, 2)
        own = pltpu.make_async_copy(wv_ref, all_ref.at[di], cross.at[4])
        own.start()

        def along(j, step, slot):
            index = j if step > 0 else half + j
            return pltpu.make_async_remote_copy(
                src_ref=wv_ref if j == 0 else all_ref.at[slot],
                dst_ref=all_ref.at[slot],
                send_sem=send_a.at[index],
                recv_sem=recv_a.at[index],
                device_id={"dp": di + 2 * step},
                device_id_type=MESH,
            )

        def across(j, step, slot):
            index = j if step > 0 else half + j
            return pltpu.make_async_remote_copy(
                src_ref=wv_ref if j == 0 else all_ref.at[slot],
                dst_ref=all_ref.at[slot],
                send_sem=send_b.at[index],
                recv_sem=recv_b.at[index],
                device_id={"dp": partner},
                device_id_type=MESH,
            )

        def has_next(step):
            return line < half - 1 if step > 0 else line > 0

        def has_slot(j, step):
            return line >= j if step > 0 else line + j < half

        across(0, 1, di).start()
        for step in (1, -1):
            pl.when(has_next(step))(lambda step=step: along(0, step, di).start())
        got_ref[...] = jnp.zeros_like(got_ref)
        for j in range(1, half):
            for step in (1, -1):

                @pl.when(has_slot(j, step))
                def _(j=j, step=step):
                    slot = di - 2 * j * step
                    along(j - 1, step, slot).wait_recv()
                    across(j, step, slot).start()
                    pl.when(has_next(step))(lambda: along(j, step, slot).start())

        own.wait()
        across(0, 1, partner).wait()
        for step in (1, -1):
            pl.when(has_next(step))(lambda step=step: along(0, step, di).wait_send())
        for j in range(1, half):
            for step in (1, -1):

                @pl.when(has_slot(j, step))
                def _(j=j, step=step):
                    slot = di - 2 * j * step
                    across(j, step, partner - 2 * j * step).wait_recv()
                    across(j, step, slot).wait_send()
                    pl.when(has_next(step))(lambda: along(j, step, slot).wait_send())

        weight_up.wait_send()
        picks_down.wait_recv()


def opening(x, wv, wo, picks, cid):
    sizes = (lax.axis_size("dp"), lax.axis_size("tensor"))
    n, n_dp = math.prod(sizes), sizes[0]
    shape = jax.ShapeDtypeStruct
    hbm = pl.BlockSpec(memory_space=pl.ANY)
    return pl.pallas_call(
        functools.partial(opening_kernel, sizes),
        out_shape=(
            shape(x.shape, x.dtype),
            shape((n_dp,) + wv.shape, wv.dtype),
            shape((wo.shape[0] // 2, wo.shape[1]), wo.dtype),
            shape(picks.shape, picks.dtype),
        ),
        in_specs=vmem(1) + [hbm, hbm] + vmem(1),
        out_specs=tuple(vmem(1) + [hbm, hbm] + vmem(1)),
        scratch_shapes=[pltpu.SemaphoreType.DMA((n,)) for _ in range(2)]
        + [pltpu.SemaphoreType.DMA((n_dp,)) for _ in range(4)]
        + [pltpu.SemaphoreType.DMA((5,))],
        compiler_params=pltpu.CompilerParams(
            collective_id=cid, has_side_effects=True, vmem_limit_bytes=58 * 1024 * 1024
        ),
    )(x, wv, wo, picks)


def relay_kernel(n, x_ref, out_ref, send_sem, recv_sem, down_sem):
    ti = lax.axis_index("tensor")
    section = lax.axis_index("section")
    barrier = pltpu.get_barrier_semaphore()
    pl.semaphore_signal(
        barrier, inc=1, device_id={"section": 1 - section}, device_id_type=MESH
    )

    @each_peer(n)
    def _(k):
        pl.semaphore_signal(
            barrier, inc=1, device_id={"tensor": lax.rem(ti + k, n)}, device_id_type=MESH
        )

    pl.semaphore_wait(barrier, n)
    down = pltpu.make_async_remote_copy(
        src_ref=x_ref,
        dst_ref=out_ref.at[ti],
        send_sem=down_sem.at[0],
        recv_sem=down_sem.at[1],
        device_id={"section": 0},
        device_id_type=MESH,
    )
    coords = lambda index: {"tensor": index}

    @pl.when(section == 1)
    def _():
        down.start()
        out_ref[ti] = x_ref[...]
        push_all(ti, coords, n, lambda to: x_ref, out_ref, send_sem, recv_sem)
        down.wait_send()

    @pl.when(section == 0)
    def _():
        down.wait_recv()
        push_all(ti, coords, n, lambda to: out_ref.at[ti], out_ref, send_sem, recv_sem)


def relay(x, cid):
    n = lax.axis_size("tensor")
    return pl.pallas_call(
        functools.partial(relay_kernel, n),
        out_shape=jax.ShapeDtypeStruct((n,) + x.shape, x.dtype),
        in_specs=vmem(1),
        out_specs=vmem(1)[0],
        scratch_shapes=[pltpu.SemaphoreType.DMA((max(n, 2),)) for _ in range(3)],
        **params(cid, x, jax.ShapeDtypeStruct((n,) + x.shape, x.dtype)),
    )(x)


def scatter_kernel(n, x_ref, out_ref, held, send_a, recv_a, down_sem):
    me, coords = place(("dp",), (n,))
    section = lax.axis_index("section")
    barrier = pltpu.get_barrier_semaphore()
    pl.semaphore_signal(
        barrier, inc=1, device_id={"section": 1 - section}, device_id_type=MESH
    )

    @each_peer(n)
    def _(k):
        pl.semaphore_signal(
            barrier, inc=1, device_id=coords(lax.rem(me + k, n)), device_id_type=MESH
        )

    pl.semaphore_wait(barrier, n)
    held[me] = x_ref[me]
    push_all(me, coords, n, lambda to: x_ref.at[to], held, send_a, recv_a)
    out_ref[section] = jnp.sum(held[...].astype(F32), axis=0).astype(out_ref.dtype)
    down = pltpu.make_async_remote_copy(
        src_ref=out_ref.at[1],
        dst_ref=out_ref.at[1],
        send_sem=down_sem.at[0],
        recv_sem=down_sem.at[1],
        device_id={"section": 0},
        device_id_type=MESH,
    )

    @pl.when(section == 1)
    def _():
        out_ref[0] = jnp.zeros_like(out_ref[0])
        down.start()
        down.wait_send()

    @pl.when(section == 0)
    def _():
        down.wait_recv()


def scatter(x, cid):
    n = lax.axis_size("dp")
    return pl.pallas_call(
        functools.partial(scatter_kernel, n),
        out_shape=jax.ShapeDtypeStruct((2,) + x.shape[1:], x.dtype),
        in_specs=vmem(1),
        out_specs=vmem(1)[0],
        scratch_shapes=[pltpu.VMEM(x.shape, x.dtype)]
        + [pltpu.SemaphoreType.DMA((n,)) for _ in range(2)]
        + [pltpu.SemaphoreType.DMA((2,))],
        **params(cid, x, x, x),
    )(x)


def on_device(
    section_layer_input,
    value_projection_weight,
    adapter_down_weight,
    adapter_up_weight,
    output_weight,
    rotated_query_cache,
    rotated_key_cache,
    query_embedding,
    positives,
    hard_negative_passages,
    lengths,
):
    n_dp, n_tensor = lax.axis_size("dp"), lax.axis_size("tensor")
    is_top = lax.axis_index("section") == 1
    ti, di = lax.axis_index("tensor"), lax.axis_index("dp")
    x = section_layer_input[0]
    wv, down, up, wo = (
        value_projection_weight[0],
        adapter_down_weight[0],
        adapter_up_weight[0],
        output_weight[0],
    )
    rows, width = x.shape
    seqs = lengths.shape[0]
    toks = rows * n_tensor
    seq_len = toks // seqs
    cols = wv.shape[0]
    kv_cols = wv.shape[1]
    kv = kv_cols // HEAD_SIZE
    group = QH // KEY_VALUE_HEADS
    heads = kv * group
    rank = down.shape[1]
    own_q = query_embedding.shape[0]
    n_neg = hard_negative_passages.shape[1]
    n_q, n_p = n_dp * own_q, n_dp * seqs
    own_p = max(1, rows // seq_len)
    share = n_tensor * own_p // seqs
    own_first = ti * rows // seq_len

    down_cols = lax.dynamic_slice_in_dim(down, di * cols, cols, 0)
    wvf = (
        wv.astype(F32) + adapter_scale * jnp.dot(down_cols, up, preferred_element_type=F32)
    ).astype(BF16)
    wv_heads = wvf.reshape(cols, kv, HEAD_SIZE)
    half_cols = wo.shape[0] // 2

    positions = jnp.arange(seq_len, dtype=jnp.int32)
    is_valid = positions[None, :] < lengths[:, None]
    last_pick = (positions[None, :] == lengths[:, None] - 1).astype(BF16)
    query_grid = rotated_query_cache[0].reshape(seqs, seq_len, kv, group, HEAD_SIZE)
    key_grid = rotated_key_cache[0].reshape(seqs, seq_len, kv, HEAD_SIZE)
    last_query = jnp.einsum(
        "pt,pthd->phd",
        last_pick,
        rotated_query_cache[0].reshape(seqs, seq_len, heads, HEAD_SIZE),
        preferred_element_type=F32,
    ).astype(BF16)
    scores = jnp.einsum(
        "pkgd,ptkd->pkgt",
        last_query.reshape(seqs, kv, group, HEAD_SIZE),
        key_grid,
        preferred_element_type=F32,
    ) / math.sqrt(HEAD_SIZE)
    scores = jnp.where(is_valid[:, None, None, :], scores, very_low)
    probs_top = jax.nn.softmax(scores, axis=-1).astype(BF16)
    low = jnp.dot(x, down, preferred_element_type=F32).astype(BF16)
    probs_rows = probs_top.reshape(seqs * heads, seq_len)
    pad_rows = round_up(seqs * heads, 16)
    probs_rows = jnp.pad(probs_rows, ((0, pad_rows - seqs * heads), (0, 0)))
    low_rows = jnp.pad(low, ((0, 0), (0, seq_len - rank)))
    probs_all = exchange(
        jnp.concatenate([probs_rows, low_rows], axis=0), ("tensor",), 0, same=True
    )
    low_all = probs_all[:, pad_rows : pad_rows + rows, :rank].reshape(toks, rank)
    probs_all = probs_all[:, : seqs * heads]
    probs_all = probs_all.reshape(n_tensor, seqs, heads, seq_len).transpose(1, 0, 2, 3)
    picks = jnp.concatenate(
        [probs_all.reshape(seqs, QH, seq_len), last_pick[:, None, :]], axis=1
    )

    def fold():
        scores_low = jnp.einsum(
            "ptkgd,pukd->pkgtu", query_grid, key_grid, preferred_element_type=F32
        ) / math.sqrt(HEAD_SIZE)
        allowed = (positions[None, :, None] >= positions[None, None, :]) & is_valid[:, None, :]
        scores_low = jnp.where(allowed[:, None, None, :, :], scores_low, very_low)
        probs_low = jax.nn.softmax(scores_low, axis=-1).astype(BF16)
        return jnp.einsum(
            "pkgtu,pet->pkgue", probs_low, picks_above, preferred_element_type=F32
        ).astype(BF16)

    def bottom_fold():
        shape = (seqs, kv, group, seq_len, QH + 1)
        return lax.cond(is_top, lambda: jnp.zeros(shape, BF16), fold)

    def own_rows_of(full):
        part = lax.dynamic_slice_in_dim(full, own_first, own_p, 0)
        if share > 1:
            part = lax.dynamic_slice_in_dim(part, (ti % share) * rows, rows, 2)
        return part

    own_picks = own_rows_of(picks)
    picked = jnp.einsum(
        "pet,ptd->ped",
        own_picks,
        x.reshape(own_p, rows // own_p, width),
        preferred_element_type=F32,
    ).astype(BF16)
    by_block = picked.reshape(own_p, QH + 1, n_dp, cols).transpose(2, 0, 1, 3)
    head_part = by_block[:, :, :QH].reshape(n_dp, own_p, n_tensor, heads, cols)
    head_part = head_part.transpose(0, 2, 1, 3, 4).reshape(n_dp, n_tensor, own_p * heads, cols)
    last_part = by_block[:, :, QH]
    query_part = query_embedding.reshape(own_q, n_dp, cols).transpose(1, 0, 2)
    numbers = jnp.concatenate([positives[:, None], hard_negative_passages], axis=1)
    numbers = jnp.pad(numbers.astype(BF16), ((0, 0), (0, cols - 1 - n_neg)))
    numbers = jnp.broadcast_to(numbers[None], (n_dp, own_q, cols))
    tail = jnp.concatenate([last_part, query_part, numbers], axis=1)
    tail = jnp.broadcast_to(tail[:, None], (n_dp, n_tensor) + tail.shape[1:])
    message = jnp.concatenate([head_part, tail], axis=2)
    used = message.shape[2]
    message = jnp.pad(message, ((0, 0), (0, 0), (0, round_up(used, 16) - used), (0, 0)))
    pad_picks = jnp.pad(picks, ((0, 0), (0, round_up(QH + 1, 16) - QH - 1), (0, 0)))
    got, wv_all, wo_below, picks_above = opening(
        message.reshape((n_dp * n_tensor,) + message.shape[2:]), wvf, wo, pad_picks, 1
    )
    wv_all = wv_all.reshape(width, kv_cols)
    picks_above = picks_above[:, : QH + 1]
    got = got.reshape((n_dp, n_tensor) + got.shape[1:])
    first = own_p * heads

    def by_passage(part, count):
        part = part.reshape(n_dp, n_tensor // share, share, own_p, count, cols)
        if share > 1:
            part = jnp.sum(part.astype(F32), axis=2).astype(BF16)
        return part.reshape(n_p, count, cols)

    picked_all = by_passage(got[:, :, :first], heads).reshape(n_p, kv, group, cols)
    last_in = by_passage(got[:, :, first : first + own_p], 1)[:, 0].astype(F32)
    queries = got[:, 0, first + own_p : first + own_p + own_q].reshape(n_q, cols)
    numbers = got[:, 0, first + own_p + own_q : first + own_p + 2 * own_q].reshape(n_q, cols)
    all_pos = numbers[:, 0].astype(jnp.int32)
    all_neg = numbers[:, 1 : 1 + n_neg].astype(jnp.int32)

    attended = jnp.einsum("pkgd,dkc->pkgc", picked_all, wv_heads, preferred_element_type=F32)
    picked_low = jnp.einsum("pkgd,da->pkga", picked_all, down_cols, preferred_element_type=F32)
    attended, picked_low = total([attended, picked_low], ("dp",), 2, 1, BF16)
    attended = attended.reshape(n_p, heads * HEAD_SIZE).astype(BF16)
    mixed = jnp.dot(attended, wo, preferred_element_type=F32)
    mixed_rows = jnp.pad(mixed, ((0, round_up(n_p, 8) - n_p), (0, 0)))
    mixed = jnp.sum(exchange(mixed_rows, ("tensor",), 3, same=True, section=1), axis=0)[:n_p]
    pooled = last_in + mixed

    query_f = queries.astype(F32)
    pooled_hi = pooled.astype(BF16)
    pooled_lo = (pooled - pooled_hi.astype(F32)).astype(BF16)
    products = lax.dot_general(
        jnp.concatenate([queries, pooled_hi, pooled_lo], axis=0),
        wo,
        (((1,), (1,)), ((), ())),
        preferred_element_type=F32,
    )
    prod_q = products[:n_q]
    prod_p = products[n_q : n_q + n_p] + products[n_q + n_p :]
    dots = jnp.dot(query_f, pooled.T, precision=HIGH)
    prod_q, prod_p, dots, query_sq, pooled_sq = total(
        [prod_q, prod_p, dots, jnp.sum(query_f * query_f, -1), jnp.sum(pooled * pooled, -1)],
        ("dp",),
        4,
        1,
    )
    query_norm = jnp.sqrt(query_sq + tiny_eps)[:, None]
    pooled_norm = jnp.sqrt(pooled_sq + tiny_eps)[None, :]
    cosines = dots / query_norm / pooled_norm
    logits = cosines / tau_value
    passage_ids = jnp.arange(n_p, dtype=jnp.int32)
    pos_hot = (all_pos[:, None] == passage_ids[None, :]).astype(F32)
    is_positive = jnp.any(all_pos[:, None] == passage_ids[None, :], axis=0)
    is_negative = jnp.any(all_neg[:, :, None] == passage_ids[None, None, :], axis=1)
    candidate = is_positive[None, :] | is_negative
    row_max = jnp.max(jnp.where(candidate, logits, very_low), axis=-1)
    row_total = jnp.sum(jnp.where(candidate, jnp.exp(logits - row_max[:, None]), 0.0), axis=-1)
    row_lse = row_max + jnp.log(row_total)
    all_loss = row_lse - jnp.sum(pos_hot * logits, axis=-1)
    weights = jnp.where(candidate, jnp.exp(logits - row_lse[:, None]), 0.0) - pos_hot
    weights = weights * (loss_scale / (n_q * tau_value))
    along = jnp.sum(weights * cosines, axis=0)
    norm = pooled_norm[0][:, None]
    coef_q = (weights / query_norm).T / norm
    coef_p = along[:, None] / (norm * norm)
    grad_pool = (jnp.dot(coef_q, query_f, precision=HIGH) - coef_p * pooled).astype(BF16)
    grad_att = (jnp.dot(coef_q, prod_q, precision=HIGH) - coef_p * prod_p).astype(BF16)

    grad_heads = grad_att.reshape(n_p, kv, group, HEAD_SIZE)
    pulled = jnp.einsum("pkgc,dkc->pkgd", grad_heads, wv_heads, preferred_element_type=F32)
    pulled = pulled.astype(BF16).reshape(n_p, heads, cols)
    to_send = jnp.concatenate([pulled.reshape(n_p * heads, cols), grad_pool], axis=0)
    to_send = jnp.pad(to_send, ((0, round_up(to_send.shape[0], 16) - to_send.shape[0]), (0, 0)))
    pulled = jnp.concatenate([pulled, grad_pool[:, None, :]], axis=1)
    pulled = pulled.reshape(n_dp, n_tensor // share, own_p * (heads + 1), cols)
    used = own_p * (heads + 1)
    pulled = jnp.pad(pulled, ((0, 0), (0, 0), (0, round_up(used, 16) - used), (0, 0)))
    pulled = jnp.repeat(pulled, share, axis=1)
    own_pulled = exchange(
        pulled.reshape((n_dp * n_tensor,) + pulled.shape[2:]), ("dp", "tensor"), 6, section=1
    )[:, :used]
    own_pulled = own_pulled.reshape(n_dp, n_tensor, own_p, heads + 1, cols)
    pulled_heads = own_pulled[:, :, :, :heads].transpose(2, 1, 3, 0, 4).reshape(own_p, QH, width)
    pulled_last = own_pulled[:, 0, :, heads].transpose(1, 0, 2).reshape(own_p, 1, width)
    pulled_rows = jnp.concatenate([pulled_heads, pulled_last], axis=1)
    folded = bottom_fold()
    to_send, folded, own_rows = lax.optimization_barrier((to_send, folded, pulled_rows))
    from_group = relay(to_send, 5)
    from_group, pulled_rows, all_loss = lax.optimization_barrier(
        (from_group, own_rows, all_loss)
    )
    pulled_below = lax.ppermute(pulled_rows, "section", [(1, 0)])

    above_heads = from_group[:, : n_p * heads].reshape(n_tensor, n_p, heads, cols)
    above_heads = above_heads.transpose(1, 0, 2, 3).reshape(n_p, QH, cols)
    above_pool = from_group[0, n_p * heads : n_p * heads + n_p]
    above_rows = jnp.concatenate([above_heads, above_pool[:, None, :]], axis=1)
    spread = lax.dot_general(
        above_rows.reshape(n_p * (QH + 1), cols),
        jnp.where(is_top, wo_below, wo[:half_cols]),
        (((1,), (1,)), ((), ())),
        preferred_element_type=F32,
    ).astype(BF16)
    spread = spread.reshape(n_dp, -1, 128)
    used = spread.shape[1]
    spread = jnp.pad(spread, ((0, 0), (0, round_up(used, 16) - used), (0, 0)))
    spread = scatter(spread, 10)[:, :used].reshape(2, seqs * (QH + 1), half_cols)
    spread = jnp.concatenate([spread[0], spread[1]], axis=1)
    spread = spread.reshape(seqs, QH + 1, kv, group, HEAD_SIZE)

    own_above = own_rows_of(picks_above)
    grad_top = jnp.einsum(
        "pet,ped->ptd",
        jnp.where(is_top, own_picks, own_above),
        jnp.where(is_top, pulled_rows, pulled_below),
        preferred_element_type=F32,
    )
    grad_top = grad_top.astype(BF16).reshape(rows, width)
    up_heads = up.reshape(rank, kv, HEAD_SIZE)
    up_top = adapter_scale * jnp.einsum(
        "pkga,pkgc->akc", picked_low.astype(BF16), grad_heads, preferred_element_type=F32
    ).reshape(rank, kv_cols)
    back_top = jnp.einsum(
        "pkgc,akc->pkga", grad_heads, up_heads, preferred_element_type=F32
    ).astype(BF16)
    down_top = adapter_scale * jnp.einsum(
        "pkga,pkgd->ad", back_top, picked_all, preferred_element_type=F32
    )

    grad_values = jnp.einsum(
        "pkgue,pekgc->pukc", folded, spread, preferred_element_type=F32
    ).astype(BF16)
    grad_values = grad_values.reshape(toks, kv_cols)
    term = lax.dot_general(
        grad_values, wv_all, (((1,), (1,)), ((), ())), preferred_element_type=F32
    ).astype(BF16)
    back = lax.dot_general(
        grad_values, up, (((1,), (1,)), ((), ())), preferred_element_type=F32
    ).astype(BF16)
    parts = exchange(
        jnp.concatenate([term, jnp.pad(back, ((0, 0), (0, 128 - rank)))], axis=1).reshape(
            n_tensor, rows, width + 128
        ),
        ("tensor",),
        7,
        section=0,
    )
    parts = jnp.sum(parts.astype(F32), axis=0)
    grad_bottom = (parts[:, :width] + grad_top.astype(F32)).astype(BF16)
    back_own = parts[:, width : width + rank].astype(BF16)
    down_low = adapter_scale * lax.dot_general(
        back_own, x, (((0,), (0,)), ((), ())), preferred_element_type=F32
    )
    up_low = adapter_scale * lax.dot_general(
        low_all, grad_values, (((0,), (0,)), ((), ())), preferred_element_type=F32
    )

    grad_input = jnp.where(is_top, grad_top, grad_bottom)
    down_top = lax.dynamic_update_slice_in_dim(
        jnp.zeros((rank, width), F32), down_top, di * cols, 1
    )
    grad_down = jnp.where(is_top, down_top, down_low)
    grad_up = jnp.where(is_top, jnp.where(di == 0, up_top, 0.0), up_low)
    ups = lax.dynamic_update_slice_in_dim(
        jnp.zeros((n_tensor, rank, kv_cols), F32), grad_up[None], ti, 0
    )
    grad_down, ups = total([grad_down, ups], ("dp", "tensor"), 8, None, BF16)
    grad_down, ups = grad_down.T.astype(F32), ups.astype(F32)
    grad_up = lax.dynamic_slice_in_dim(ups, ti, 1, 0)
    own_loss = lax.dynamic_slice_in_dim(all_loss, di * own_q, own_q, 0)
    below_loss = lax.ppermute(own_loss, "section", [(1, 0)])
    query_loss = jnp.where(is_top, own_loss, below_loss)
    return (query_loss, grad_input[None], grad_down[None], grad_up)


def solution(mesh):
    return jax.shard_map(
        on_device,
        mesh=mesh,
        in_specs=(
            P("section", ("dp", "tensor"), None),
            P("section", "dp", "tensor"),
            P("section", None, None),
            P("section", None, "tensor"),
            P("section", "tensor", "dp"),
            P("section", "dp", "tensor"),
            P("section", "dp", "tensor"),
            P("dp", None),
            P("dp"),
            P("dp", None),
            P("dp"),
        ),
        out_specs=(
            P("dp"),
            P("section", ("dp", "tensor"), None),
            P("section", None, None),
            P("section", None, "tensor"),
        ),
        check_vma=False,
    )
```
